128 devices in a mesh: ctx: 32 (over y, x_lo, z), fsdp: 4 (over x_hi, core).
Axes of the slice: x: 4 (x_hi: 2, x_lo: 2; x = x_hi * 2 + x_lo), y: 4, z: 4, core: 2. Of those that a mesh axis runs over, the one named last changes fastest.
Arguments:
- tokens: bfloat16 [4, 4096, 960], P('fsdp', 'ctx'), may hold values from -6 to 6
- pair_table: int32 [32], replicated, may hold values from 0 to 31, each once
- gain_attn: float32 [960], replicated, may hold values from 0.1 to 1.9
- w_query: bfloat16 [960, 960], P('fsdp', 'ctx'), may hold values from -0.1875 to 0.1875
- w_key: bfloat16 [960, 320], P('fsdp', 'ctx'), may hold values from -0.1875 to 0.1875
- w_value: bfloat16 [960, 320], P('fsdp', 'ctx'), may hold values from -0.1875 to 0.1875
- w_out: bfloat16 [960, 960], P('fsdp', 'ctx'), may hold values from -3.5 to 3.5
- gain_mlp: float32 [960], replicated, may hold values from 0.1 to 1.9
- w_gate: bfloat16 [960, 2560], P('fsdp', 'ctx'), may hold values from -0.1875 to 0.1875
- w_up: bfloat16 [960, 2560], P('fsdp', 'ctx'), may hold values from -0.1875 to 0.1875
- w_down: bfloat16 [2560, 960], P('fsdp', 'ctx'), may hold values from -0.125 to 0.125
- cotangent: bfloat16 [4, 4096, 960], P('fsdp', 'ctx'), may hold values from -6 to 6
Outputs:
- result: bfloat16 [4, 4096, 960], P('fsdp', 'ctx')
- grad_tokens: float32 [4, 4096, 960], P('fsdp', 'ctx')
- grad_gain_attn: float32 [960], replicated
- grad_w_query: float32 [960, 960], P('fsdp', 'ctx')
- grad_w_key: float32 [960, 320], P('fsdp', 'ctx')
- grad_w_value: float32 [960, 320], P('fsdp', 'ctx')
- grad_w_out: float32 [960, 960], P('fsdp', 'ctx')
- grad_gain_mlp: float32 [960], replicated
- grad_w_gate: float32 [960, 2560], P('fsdp', 'ctx')
- grad_w_up: float32 [960, 2560], P('fsdp', 'ctx')
- grad_w_down: float32 [2560, 960], P('fsdp', 'ctx')
The draws below stay inside these ranges and needn't reach their ends.
Inputs may be any that keep to these rules, and one draw needn't show every extreme that they name: A permutation of the indices of ctx; index c holds the sequence blocks pair_table[c] and 63 - pair_table[c], each of 64 tokens.
All inputs are finite; a program needn't handle non-finite values.
Results may differ from the reference program's by a relative error of at most 0.035.
Values may be sent and summed in bfloat16 or wider, within the bound.
No kernel may reach another device: no remote copies, remote signals or barrier semaphores. Data moves between devices by JAX's collectives and lax.ppermute only.
A program may use at most 128 MiB of HBM per device.

```python
import math
import jax
import jax.numpy as jnp
from jax import lax

D = 960
QUERY_HEADS = 15
KEY_VALUE_HEADS = 5
HEAD_WIDTH = 64
FF = 2560
TOK_DEV = 128
SEQ = 4096
SEQS = 4
KV = 320
N_CTX = 32


def levels(stream_key, dims, pieces, least, high):
    gain = 1.0
    for position, shards_of in pieces:
        heights = jax.random.uniform(jax.random.fold_in(jax.random.fold_in(stream_key, 6), position), (shards_of,), jnp.float32, least / len(pieces), high / len(pieces))
        gain = gain * jnp.repeat(jnp.exp(heights), dims[position] // shards_of).reshape((-1,) + (1,) * (len(dims) - 1 - position))
    return gain


def scatter_about(stream_key, dims, width, most, pieces=(), kind=jnp.bfloat16):
    gain = levels(stream_key, dims, pieces, -0.22, 0.18) if pieces else 1.0
    result = jax.random.normal(stream_key, dims, jnp.float32) * width * gain
    return jnp.minimum(jnp.maximum(result, -most), most).astype(kind)


def setup_inputs(seed: int = 0) -> dict:
    keys = jax.random.split(jax.random.key(seed), 13)
    tokens = scatter_about(keys[0], (SEQS, SEQ, D), 1.0, 6.0, ((0, 4), (1, 32)))
    pair_table = jax.random.permutation(keys[1], N_CTX).astype(jnp.int32)
    gain_attn = jnp.clip(1.0 + 0.18 * jax.random.normal(keys[2], (D,), jnp.float32), 0.1, 1.9)
    w_query = scatter_about(keys[3], (D, D), D ** -0.5, 0.1875, ((0, 4), (1, 32)))
    w_key = scatter_about(keys[4], (D, KV), D ** -0.5, 0.1875, ((0, 4), (1, 32)))
    w_value = scatter_about(keys[5], (D, KV), D ** -0.5, 0.1875, ((0, 4), (1, 32)))
    w_out = scatter_about(keys[6], (D, D), (max(1, 16 * D // (TOK_DEV * N_CTX))) ** -0.5, 3.5, ((0, 4), (1, 32)))
    gain_mlp = jnp.clip(1.0 + 0.18 * jax.random.normal(keys[7], (D,), jnp.float32), 0.1, 1.9)
    w_gate = scatter_about(keys[8], (D, FF), D ** -0.5, 0.1875, ((0, 4), (1, 32)))
    w_up = scatter_about(keys[9], (D, FF), D ** -0.5, 0.1875, ((0, 4), (1, 32)))
    w_down = scatter_about(keys[10], (FF, D), FF ** -0.5, 0.125, ((0, 4), (1, 32)))
    cotangent = scatter_about(keys[11], (SEQS, SEQ, D), 1.0, 6.0, ((0, 4), (1, 32)))
    return {"tokens": tokens, "pair_table": pair_table, "gain_attn": gain_attn, "w_query": w_query, "w_key": w_key, "w_value": w_value, "w_out": w_out, "gain_mlp": gain_mlp, "w_gate": w_gate, "w_up": w_up, "w_down": w_down, "cotangent": cotangent}


EPSILON = 1e-05
THETA = 10000.0
HIGHEST = lax.Precision.HIGHEST

@jax.custom_vjp
def low(v):
    return lax.optimization_barrier(v.astype(jnp.bfloat16)).astype(jnp.float32)

@jax.custom_vjp
def low_back(v):
    return v

def low_keep(v):
    return (low(v), None)

def low_pass(kept, grad):
    return (grad,)

def back_keep(v):
    return (v, None)

def back_low(kept, grad):
    return (low(grad),)
low.defvjp(low_keep, low_pass)
low_back.defvjp(back_keep, back_low)

def token_positions(pair_table, rows_per_block, ctx_count):
    sequence_length = rows_per_block * ctx_count
    row_index = jnp.arange(sequence_length, dtype=jnp.int32)
    owner_index = row_index // rows_per_block
    within = row_index % rows_per_block
    half_rows = rows_per_block // 2
    matches = (owner_index[:, None] == jnp.arange(ctx_count, dtype=jnp.int32)[None, :]).astype(jnp.int32)
    paired = lax.optimization_barrier(jnp.sum(matches * pair_table[None, :], axis=1, dtype=jnp.int32))
    blocks = jnp.where(within < half_rows, paired, 2 * ctx_count - 1 - paired)
    return (blocks * half_rows + within % half_rows).astype(jnp.int32)

def rope_tables(positions, head_size):
    half_size = head_size // 2
    frequencies = THETA ** (-2.0 * jnp.arange(half_size, dtype=jnp.float32) / head_size)
    angles = positions.astype(jnp.float32)[:, None] * frequencies[None, :]
    cosine = jnp.cos(angles)
    sine_part = jnp.sin(angles)
    cosine_lookup = jnp.concatenate([cosine, cosine], axis=1)[:, None, :]
    sine_lookup = jnp.concatenate([sine_part, sine_part], axis=1)[:, None, :]
    return (cosine_lookup, sine_lookup)

def apply_rotary(head_rows, cosine_lookup, sine_lookup):
    half_size = head_rows.shape[-1] // 2
    turned = jnp.concatenate([-head_rows[..., half_size:], head_rows[..., :half_size]], axis=-1)
    return head_rows * cosine_lookup + turned * sine_lookup

def attend_block(query_row_block, query_pos, key_head_split, value_head_split, key_pos):
    rows_per_block = query_row_block.shape[0]
    grouped_queries = query_row_block.reshape(rows_per_block, KEY_VALUE_HEADS, QUERY_HEADS // KEY_VALUE_HEADS, HEAD_WIDTH)
    raw_scores = low_back(jnp.einsum('tkgd,skd->kgts', grouped_queries, key_head_split, precision=HIGHEST))
    visible = key_pos[None, :] <= query_pos[:, None]
    scores = jnp.where(visible, raw_scores * (1.0 / math.sqrt(HEAD_WIDTH)), -1e+30)
    row_top = lax.optimization_barrier(jnp.max(scores, axis=-1, keepdims=True))
    weights = jnp.where(visible, jnp.exp(scores - row_top), 0.0)
    probabilities = weights / lax.optimization_barrier(jnp.sum(weights, axis=-1, keepdims=True))
    mixture = jnp.einsum('kgts,skd->tkgd', low(probabilities), value_head_split, precision=HIGHEST)
    return mixture.reshape(rows_per_block, QUERY_HEADS * HEAD_WIDTH)

def layer(hidden_in, parameters, cosine_lookup, sine_lookup, positions):
    gain_attn, w_query, w_key, w_value, w_out, gain_mlp, w_gate, w_up, w_down = parameters
    sequence_length = hidden_in.shape[0]
    inverse_one = lax.rsqrt(lax.optimization_barrier(jnp.mean(hidden_in * hidden_in, axis=-1, keepdims=True)) + EPSILON)
    normed_one = low(hidden_in * inverse_one * gain_attn)
    query_rows = low_back(jnp.dot(normed_one, w_query, precision=HIGHEST))
    key_row_block = low_back(jnp.dot(normed_one, w_key, precision=HIGHEST))
    value_row_block = low(low_back(jnp.dot(normed_one, w_value, precision=HIGHEST)))
    turned_queries = low(apply_rotary(query_rows.reshape(sequence_length, QUERY_HEADS, HEAD_WIDTH), cosine_lookup, sine_lookup))
    rotated_keys = low(apply_rotary(key_row_block.reshape(sequence_length, KEY_VALUE_HEADS, HEAD_WIDTH), cosine_lookup, sine_lookup))
    value_head_split = value_row_block.reshape(sequence_length, KEY_VALUE_HEADS, HEAD_WIDTH)
    rows_per_block = math.gcd(sequence_length, 512)
    block_count = sequence_length // rows_per_block

    def one_block(block_pair):
        return attend_block(block_pair[0], block_pair[1], rotated_keys, value_head_split, positions)
    mixture = lax.map(jax.checkpoint(one_block), (turned_queries.reshape(block_count, rows_per_block, QUERY_HEADS, HEAD_WIDTH), positions.reshape(block_count, rows_per_block)))
    attended = low(low_back(mixture.reshape(sequence_length, QUERY_HEADS * HEAD_WIDTH)))
    branch_one = low_back(jnp.dot(attended, w_out, precision=HIGHEST))
    middle = hidden_in + branch_one
    inverse_two = lax.rsqrt(lax.optimization_barrier(jnp.mean(middle * middle, axis=-1, keepdims=True)) + EPSILON)
    normed_two = low(middle * inverse_two * gain_mlp)
    gate_values = low_back(jnp.dot(normed_two, w_gate, precision=HIGHEST))
    up_values = low_back(jnp.dot(normed_two, w_up, precision=HIGHEST))
    hidden_units = low(jax.nn.silu(gate_values) * up_values)
    branch_two = low_back(jnp.dot(hidden_units, w_down, precision=HIGHEST))
    return middle + branch_two

def reference(tokens, pair_table, gain_attn, w_query, w_key, w_value, w_out, gain_mlp, w_gate, w_up, w_down, cotangent):
    positions = token_positions(pair_table, TOK_DEV, N_CTX)
    cosine_lookup, sine_lookup = rope_tables(positions, HEAD_WIDTH)
    parameters = (gain_attn.astype(jnp.float32), w_query.astype(jnp.float32), w_key.astype(jnp.float32), w_value.astype(jnp.float32), w_out.astype(jnp.float32), gain_mlp.astype(jnp.float32), w_gate.astype(jnp.float32), w_up.astype(jnp.float32), w_down.astype(jnp.float32))

    def forward(inputs, weights_in):

        def one_sequence(sequence):
            return layer(sequence, weights_in, cosine_lookup, sine_lookup, positions)
        return lax.map(one_sequence, inputs)
    outputs, pullback = jax.vjp(forward, tokens.astype(jnp.float32), parameters)
    grad_inputs, grads = pullback(cotangent.astype(jnp.float32))
    return (outputs.astype(jnp.bfloat16), grad_inputs, grads[0], grads[1], grads[2], grads[3], grads[4], grads[5], grads[6], grads[7], grads[8])
```

```python
import functools
import math

import jax
import jax.numpy as jnp
from jax import lax
from jax.experimental import pallas as pl
from jax.experimental.pallas import tpu as pltpu
from jax.sharding import PartitionSpec as P

QUERY_HEADS = 15
KEY_VALUE_HEADS = 5
HEAD_WIDTH = 64


EPSILON = 1e-05
THETA = 10000.0
MASK_FLOOR = -1e30


def rope_tables(positions, head_size):
    half_size = head_size // 2
    frequencies = THETA ** (-2.0 * jnp.arange(half_size, dtype=jnp.float32) / head_size)
    angles = positions.astype(jnp.float32)[:, None] * frequencies[None, :]
    cosine = jnp.cos(angles)
    sine_part = jnp.sin(angles)
    cosine_lookup = jnp.concatenate([cosine, cosine], axis=1)[:, None, :]
    sine_lookup = jnp.concatenate([sine_part, sine_part], axis=1)[:, None, :]
    return (cosine_lookup, sine_lookup)


def apply_rotary(head_rows, cosine_lookup, sine_lookup):
    half_size = head_rows.shape[-1] // 2
    turned = jnp.concatenate([-head_rows[..., half_size:], head_rows[..., :half_size]], axis=-1)
    return head_rows * cosine_lookup + turned * sine_lookup


def inverse_rotary(grad_rows, cosine_lookup, sine_lookup):
    half_size = grad_rows.shape[-1] // 2
    moved = grad_rows * sine_lookup
    turned_back = jnp.concatenate([moved[..., half_size:], -moved[..., :half_size]], axis=-1)
    return grad_rows * cosine_lookup + turned_back


AXES = ("y", "xl", "z", "xh", "core")
CTX = ("y", "xl", "z")
FSDP = ("xh", "core")


def shift(block, axis, step):
    size = lax.axis_size(axis)
    return lax.ppermute(block, axis, [(i, (i + step) % size) for i in range(size)])


def ring_gather(block, axis, halves=None):
    ahead = shift(block, axis, -1)
    behind = shift(block, axis, 1)
    if halves is None:
        return block, ahead, shift(block, axis, 2), behind
    split, join = halves
    across = join(shift(split(ahead)[0], axis, -1), shift(split(behind)[1], axis, 1))
    return block, ahead, across, behind


def ring_scatter(terms, axis, halves=None):
    own, ahead, across, behind = terms
    if halves is None:
        arrived = (
            shift(ahead, axis, 1),
            shift(behind, axis, -1),
            shift(across, axis, 2),
        )
    else:
        split, join = halves
        first, second = split(across)
        first = shift(first, axis, 1)
        second = shift(second, axis, -1)
        ahead_first, ahead_second = split(ahead)
        behind_first, behind_second = split(behind)
        arrived = (
            shift(join(add(ahead_first, first), ahead_second), axis, 1),
            shift(join(behind_first, add(behind_second, second)), axis, -1),
        )
    return add(own, *arrived)


def add(*terms):
    total = terms[0].astype(jnp.float32)
    for term in terms[1:]:
        total = total + term.astype(jnp.float32)
    return total.astype(jnp.bfloat16)


def leading_halves():
    return (lambda block: (block[:1], block[1:])), (
        lambda first, second: jnp.concatenate([first, second], axis=0)
    )


def row_halves():
    def split(block):
        half = block.shape[0] // 2
        return block[:half], block[half:]

    return split, (lambda first, second: jnp.concatenate([first, second], axis=0))


def place(blocks, axis, dim):
    index = lax.axis_index(axis)
    shape = blocks[0].shape
    whole = jnp.zeros(shape[:dim] + (4,) + shape[dim:], blocks[0].dtype)
    for j, block in enumerate(blocks):
        whole = lax.dynamic_update_index_in_dim(whole, block, (index + j) % 4, dim)
    return whole


def pick(whole, axis, dim):
    index = lax.axis_index(axis)
    return [
        lax.dynamic_index_in_dim(whole, (index + j) % 4, dim, keepdims=False) for j in range(4)
    ]


def pair_gather(block, axis, dim, stack=True):
    other = shift(block, axis, 1)
    first = lax.axis_index(axis) == 0
    low = jnp.where(first, block, other)
    high = jnp.where(first, other, block)
    if stack:
        return jnp.stack([low, high], axis=dim)
    return jnp.concatenate([low, high], axis=dim)


def pair_scatter(low, high, axis):
    first = lax.axis_index(axis) == 0
    keep = jnp.where(first, low, high)
    away = jnp.where(first, high, low)
    return add(keep, shift(away, axis, 1))


def gather_y_last(block):
    pair, rows, width = block.shape
    block = place(ring_gather(block, "z"), "z", 1)
    block = pair_gather(block, "xl", 1).reshape(pair, 8 * rows, width)
    block = place(ring_gather(block, "y", leading_halves()), "y", 1)
    return block.reshape(pair, 32 * rows, width)


def scatter_y_first(block):
    pair, rows, width = block.shape
    rows = rows // 32
    block = block.reshape(pair, 4, 8 * rows, width)
    block = ring_scatter(pick(block, "y", 1), "y", leading_halves())
    block = block.reshape(pair, 2, 4, rows, width)
    block = pair_scatter(block[:, 0], block[:, 1], "xl")
    return ring_scatter(pick(block, "z", 1), "z")


def gather_z_last(block):
    pair, rows, width = block.shape
    block = pair_gather(block, "xl", 1)
    block = place(ring_gather(block, "y"), "y", 1)
    block = place(ring_gather(block, "z", leading_halves()), "z", 3)
    return block.reshape(pair, 32 * rows, width)


def scatter_z_first(block):
    pair, rows, width = block.shape
    rows = rows // 32
    block = block.reshape(pair, 4, 2, 4, rows, width)
    block = ring_scatter(pick(block, "z", 3), "z", leading_halves())
    block = ring_scatter(pick(block, "y", 1), "y")
    return pair_scatter(block[:, 0], block[:, 1], "xl")


def gather_keys(block, near, far):
    other = shift(block, "xl", 1)
    block = jnp.concatenate([block, other], axis=0)
    block = jnp.concatenate(ring_gather(block, near), axis=0)
    return jnp.concatenate(ring_gather(block, far, row_halves()), axis=0)


def scatter_keys(block, near, far):
    block = ring_scatter(jnp.split(block, 4, axis=0), far, row_halves())
    block = ring_scatter(jnp.split(block, 4, axis=0), near)
    own, other = jnp.split(block, 2, axis=0)
    return add(own, shift(other, "xl", 1))


def total_sum(block):
    for axis in ("core", "xh", "xl"):
        block = block + shift(block, axis, 1)
    for axis in ("z", "y"):
        block = (block + shift(block, axis, 2)) + (shift(block, axis, 1) + shift(block, axis, -1))
    return block


def block_table(pair_table):
    y, xl, z = (lax.axis_index(axis) for axis in CTX)
    four = jnp.arange(4, dtype=jnp.int32)
    ys = ((y + four) % 4) * 8
    zs = (z + four) % 4
    xs = ((xl + jnp.arange(2, dtype=jnp.int32)) % 2) * 4
    low = ys[:, None, None] + zs[None, :, None] + xs[None, None, :]
    high = ys[None, :, None] + zs[:, None, None] + xs[None, None, :]
    count = pair_table.shape[0]

    def paired(owners):
        matches = owners.reshape(-1)[:, None] == jnp.arange(count, dtype=jnp.int32)[None, :]
        return jnp.sum(jnp.where(matches, pair_table[None, :], 0), axis=1, dtype=jnp.int32)

    return jnp.concatenate([paired(low), 2 * count - 1 - paired(high)])


def half_columns(rows, width):
    core = lax.axis_index("core")
    parts = [rows[:, i * width : (i + 1) * width] for i in range(4)]
    even = jnp.concatenate([parts[0], parts[2]], axis=1)
    odd = jnp.concatenate([parts[1], parts[3]], axis=1)
    return jnp.where(core == 0, even, odd), jnp.where(core == 0, odd, even)


def both(rows, weights):
    return jnp.einsum(
        "td,ed->te", rows[0], weights[0], preferred_element_type=jnp.float32
    ) + jnp.einsum("td,ed->te", rows[1], weights[1], preferred_element_type=jnp.float32)


def back_through(grads, weights):
    own = jnp.einsum("te,ed->td", grads, weights[0], preferred_element_type=jnp.float32)
    other = jnp.einsum("te,ed->td", grads, weights[1], preferred_element_type=jnp.float32)
    return merge_columns(own, other)


def merge_columns(own, other):
    core = lax.axis_index("core")
    even = jnp.where(core == 0, own, other)
    odd = jnp.where(core == 0, other, own)
    width = own.shape[1] // 2
    return jnp.concatenate(
        [even[:, :width], odd[:, :width], even[:, width:], odd[:, width:]], axis=1
    )


def weight_term(left, right):
    return jnp.einsum("te,td->ed", left, right, preferred_element_type=jnp.float32).astype(
        jnp.bfloat16
    )


TILE = 512
LANES = 2 * HEAD_WIDTH


def lane_pair(part):
    return slice(part // 2 * LANES, part // 2 * LANES + LANES)


def fill_bias(base_ref, query_ref, bias_ref, half_rows):
    def step(chunk, carry):
        rows = pl.ds(chunk * half_rows, half_rows)
        position = base_ref[chunk] + lax.broadcasted_iota(jnp.int32, (half_rows, LANES), 0)
        bias_ref[rows, :] = jnp.where(position <= query_ref[...], 0.0, MASK_FLOOR)
        return carry

    lax.fori_loop(0, base_ref.shape[0], step, 0)


def tile_scores(kv_ref, rows, q_ref, bias, group):
    scores = lax.dot_general(
        kv_ref[rows, lane_pair(group)],
        q_ref[group],
        (((1,), (1,)), ((), ())),
        preferred_element_type=jnp.float32,
    )
    return scores + bias


def attend_kernel(base_ref, query_ref, kv_ref, q_ref, o_ref, lse_ref, bias_ref, *, half_rows):
    fill_bias(base_ref, query_ref, bias_ref, half_rows)
    wide = q_ref.shape[1]
    tiles = kv_ref.shape[0] // TILE
    for group in range(KEY_VALUE_HEADS):

        def step(tile, carry, group=group):
            top, total, mixed = carry
            rows = pl.ds(pl.multiple_of(tile * TILE, TILE), TILE)
            bias = jnp.concatenate([bias_ref[rows, :]] * (wide // LANES), axis=1)
            scores = tile_scores(kv_ref, rows, q_ref, bias, group)
            new_top = jnp.maximum(top, jnp.max(scores, axis=0, keepdims=True))
            factor = jnp.exp(top - new_top)
            weights = jnp.exp(scores - new_top)
            total = total * factor + jnp.sum(weights, axis=0, keepdims=True)
            mixed = mixed * factor + lax.dot_general(
                kv_ref[rows, lane_pair(KEY_VALUE_HEADS + group)],
                weights.astype(jnp.bfloat16),
                (((0,), (0,)), ((), ())),
                preferred_element_type=jnp.float32,
            )
            return new_top, total, mixed

        top, total, mixed = lax.fori_loop(
            0,
            tiles,
            step,
            (
                jnp.full((1, wide), MASK_FLOOR, jnp.float32),
                jnp.zeros((1, wide), jnp.float32),
                jnp.zeros((LANES, wide), jnp.float32),
            ),
        )
        side = (KEY_VALUE_HEADS + group) % 2 * HEAD_WIDTH
        o_ref[group] = (mixed / total)[side : side + HEAD_WIDTH]
        lse_ref[group] = top + jnp.log(total)


def backward_kernel(
    base_ref,
    query_ref,
    kv_ref,
    q_ref,
    do_ref,
    lse_ref,
    delta_ref,
    dkv_ref,
    dq_ref,
    bias_ref,
    *,
    half_rows,
):
    fill_bias(base_ref, query_ref, bias_ref, half_rows)
    wide = q_ref.shape[1]
    tiles = kv_ref.shape[0] // TILE
    dq_ref[...] = jnp.zeros_like(dq_ref)

    def step(tile, carry):
        rows = pl.ds(pl.multiple_of(tile * TILE, TILE), TILE)
        bias = jnp.concatenate([bias_ref[rows, :]] * (wide // LANES), axis=1)
        sums = [None] * KEY_VALUE_HEADS

        def collect(part, term):
            pair = part // 2
            sums[pair] = term if sums[pair] is None else sums[pair] + term

        for group in range(KEY_VALUE_HEADS):
            scores = tile_scores(kv_ref, rows, q_ref, bias, group)
            probs = jnp.exp(scores - lse_ref[group])
            grad_probs = lax.dot_general(
                kv_ref[rows, lane_pair(KEY_VALUE_HEADS + group)],
                do_ref[group],
                (((1,), (1,)), ((), ())),
                preferred_element_type=jnp.float32,
            )
            ds = (probs * (grad_probs - delta_ref[group])).astype(jnp.bfloat16)
            collect(
                KEY_VALUE_HEADS + group,
                jnp.dot(
                    probs.astype(jnp.bfloat16), do_ref[group], preferred_element_type=jnp.float32
                ),
            )
            collect(group, jnp.dot(ds, q_ref[group], preferred_element_type=jnp.float32))
            dq_ref[group] += lax.dot_general(
                kv_ref[rows, lane_pair(group)],
                ds,
                (((0,), (0,)), ((), ())),
                preferred_element_type=jnp.float32,
            )
        for pair in range(KEY_VALUE_HEADS):
            dkv_ref[rows, pair * LANES : (pair + 1) * LANES] = sums[pair].astype(jnp.bfloat16)
        return carry

    lax.fori_loop(0, tiles, step, 0)


def in_vmem():
    return pl.BlockSpec(memory_space=pltpu.VMEM)


def in_smem():
    return pl.BlockSpec(memory_space=pltpu.SMEM)


def spread_heads(rows, offset):
    count = rows.shape[0]
    heads = rows.reshape(count, KEY_VALUE_HEADS, -1, HEAD_WIDTH).transpose(1, 2, 0, 3)
    heads = heads.reshape(KEY_VALUE_HEADS, -1, HEAD_WIDTH)
    blank = jnp.zeros_like(heads)
    left = jnp.concatenate([heads, blank], axis=2)
    right = jnp.concatenate([blank, heads], axis=2)
    side = (offset + jnp.arange(KEY_VALUE_HEADS, dtype=jnp.int32)) % 2
    return jnp.where(side[:, None, None] == 0, left, right)


def join_heads(heads, count):
    heads = heads.reshape(KEY_VALUE_HEADS, HEAD_WIDTH, -1, count)
    return heads.transpose(3, 0, 2, 1).reshape(count, QUERY_HEADS * HEAD_WIDTH)


def attend(bases, query_pos, key_value, queries, half_rows):
    groups, wide, lanes = queries.shape
    keys = key_value.shape[0]
    return pl.pallas_call(
        functools.partial(attend_kernel, half_rows=half_rows),
        out_shape=(
            jax.ShapeDtypeStruct((groups, HEAD_WIDTH, wide), jnp.float32),
            jax.ShapeDtypeStruct((groups, 1, wide), jnp.float32),
        ),
        in_specs=[in_smem(), in_vmem(), in_vmem(), in_vmem()],
        out_specs=(in_vmem(), in_vmem()),
        scratch_shapes=[pltpu.VMEM((keys, lanes), jnp.float32)],
        compiler_params=pltpu.CompilerParams(vmem_limit_bytes=40 * 2**20),
        cost_estimate=pl.CostEstimate(
            flops=4 * groups * wide * lanes * keys,
            bytes_accessed=keys * 640 * 2,
            transcendentals=groups * wide * keys,
        ),
        name="attend",
    )(bases, query_pos, key_value, queries)


def attend_backward(bases, query_pos, key_value, queries, head_grads, lse, delta, half_rows):
    groups, wide, lanes = queries.shape
    keys = key_value.shape[0]
    return pl.pallas_call(
        functools.partial(backward_kernel, half_rows=half_rows),
        out_shape=(
            jax.ShapeDtypeStruct(key_value.shape, jnp.bfloat16),
            jax.ShapeDtypeStruct((groups, lanes, wide), jnp.float32),
        ),
        in_specs=[in_smem()] + [in_vmem()] * 6,
        out_specs=(in_vmem(), in_vmem()),
        scratch_shapes=[pltpu.VMEM((keys, lanes), jnp.float32)],
        compiler_params=pltpu.CompilerParams(vmem_limit_bytes=40 * 2**20),
        cost_estimate=pl.CostEstimate(
            flops=10 * groups * wide * lanes * keys,
            bytes_accessed=keys * 640 * 4,
            transcendentals=groups * wide * keys,
        ),
        name="attend_backward",
    )(bases, query_pos, key_value, queries, head_grads, lse, delta)


def body(
    tokens,
    pair_table,
    gain_attn,
    w_query,
    w_key,
    w_value,
    w_out,
    gain_mlp,
    w_gate,
    w_up,
    w_down,
    cotangent,
):
    device_rows = tokens.shape[1]
    half_rows = device_rows // 2
    width = HEAD_WIDTH * KEY_VALUE_HEADS
    query_per_group = QUERY_HEADS // KEY_VALUE_HEADS
    scale_factor = 1.0 / math.sqrt(HEAD_WIDTH)
    within = jnp.arange(half_rows, dtype=jnp.int32)
    blocks = block_table(pair_table)
    all_pos = (blocks[:, None] * half_rows + within[None, :]).reshape(-1)
    chunk_count = blocks.shape[0]
    own_pos = jnp.concatenate(
        [blocks[0] * half_rows + within, blocks[chunk_count // 2] * half_rows + within]
    )
    cosine_lookup, sine_lookup = rope_tables(own_pos, HEAD_WIDTH)

    def gather_halves(shards, gather):
        packed = jnp.stack([shard.T for shard in shards], axis=0)
        packed = pair_gather(packed, "xh", 2, stack=False)
        own = gather(packed)
        return own, shift(own, "core", 1)

    key_value_w = gather_halves((w_key, w_value), gather_y_last)
    query_out_w = gather_halves((w_query, w_out), gather_y_last)
    gate_up_w = gather_halves((w_gate, w_up), gather_z_last)
    down_own = gather_y_last(pair_gather(w_down.T, "xh", 0))
    down_w = (down_own, shift(down_own, "core", 1))
    rows_w = w_query.shape[0]
    ff_w = w_down.shape[0]

    inputs = tokens[0].astype(jnp.float32)
    inverse_one = lax.rsqrt(jnp.mean(inputs * inputs, axis=-1, keepdims=True) + EPSILON)
    normed_one = inputs * inverse_one
    rounded_one = half_columns((normed_one * gain_attn).astype(jnp.bfloat16), rows_w)
    unrotated_key = both(rounded_one, [half[0] for half in key_value_w]).reshape(
        device_rows, KEY_VALUE_HEADS, HEAD_WIDTH
    )
    value_local = both(rounded_one, [half[1] for half in key_value_w]).astype(jnp.bfloat16)
    key_local = (
        apply_rotary(unrotated_key, cosine_lookup, sine_lookup)
        .astype(jnp.bfloat16)
        .reshape(device_rows, width)
    )
    key_value = jnp.concatenate([key_local, value_local], axis=1)
    key_value_all = jnp.concatenate(
        [
            gather_keys(key_value[:half_rows], "z", "y"),
            gather_keys(key_value[half_rows:], "y", "z"),
        ],
        axis=0,
    )
    query_raw = both(rounded_one, [half[0] for half in query_out_w]).reshape(
        device_rows, QUERY_HEADS, HEAD_WIDTH
    )
    query_heads = apply_rotary(query_raw, cosine_lookup, sine_lookup).astype(jnp.bfloat16)
    queries = spread_heads(
        query_heads.reshape(device_rows, QUERY_HEADS * HEAD_WIDTH)
        * jnp.asarray(scale_factor, jnp.bfloat16),
        0,
    )
    bases = blocks * half_rows
    query_pos = own_pos[None, :]
    mixed, log_total = attend(bases, query_pos, key_value_all, queries, half_rows)
    mixture = join_heads(mixed, device_rows)
    attended = mixture.astype(jnp.bfloat16)
    out_rows = [half[1] for half in query_out_w]
    middle = inputs + both(half_columns(attended, rows_w), out_rows)
    inverse_two = lax.rsqrt(jnp.mean(middle * middle, axis=-1, keepdims=True) + EPSILON)
    normed_two = middle * inverse_two
    rounded_two = half_columns((normed_two * gain_mlp).astype(jnp.bfloat16), rows_w)
    gate_values = both(rounded_two, [half[0] for half in gate_up_w])
    up_values = both(rounded_two, [half[1] for half in gate_up_w])
    sigmoid_gate = jax.nn.sigmoid(gate_values)
    silu_gate = gate_values * sigmoid_gate
    hidden_units = half_columns((silu_gate * up_values).astype(jnp.bfloat16), ff_w)
    result = middle
    for hidden_half, down_half in zip(hidden_units, down_w):
        for i in range(2):
            result = result + jnp.einsum(
                "tf,df->td",
                hidden_half[:, i * ff_w : (i + 1) * ff_w],
                down_half[i],
                preferred_element_type=jnp.float32,
            )
    result = result.astype(jnp.bfloat16)
    grad_result = cotangent[0]
    down_terms = [
        jnp.stack(
            [weight_term(grad_result, half[:, :ff_w]), weight_term(grad_result, half[:, ff_w:])]
        )
        for half in hidden_units
    ]
    grad_down = add(down_terms[0], shift(down_terms[1], "core", 1))
    grad_down = scatter_y_first(grad_down)
    grad_down = pair_scatter(grad_down[0], grad_down[1], "xh")
    grad_hidden = merge_columns(
        *[
            jnp.concatenate(
                [
                    jnp.einsum("td,df->tf", grad_result, half[i], preferred_element_type=jnp.float32)
                    for i in range(2)
                ],
                axis=1,
            )
            for half in down_w
        ]
    )
    grad_gate_values = (
        grad_hidden * up_values * sigmoid_gate * (1.0 + gate_values * (1.0 - sigmoid_gate))
    ).astype(jnp.bfloat16)
    grad_up_values = (grad_hidden * silu_gate).astype(jnp.bfloat16)

    def scatter_halves(lefts, rights, scatter):
        terms = [
            jnp.stack([weight_term(left, half) for left, half in zip(lefts, halves)])
            for halves in rights
        ]
        term = scatter(add(terms[0], shift(terms[1], "core", 1)))
        return pair_scatter(term[..., :rows_w], term[..., rows_w:], "xh")

    grad_gate_up = scatter_halves(
        (grad_gate_values, grad_up_values), [(half, half) for half in rounded_two], scatter_z_first
    )
    grad_normed_two = back_through(grad_gate_values, [half[0] for half in gate_up_w])
    grad_normed_two = grad_normed_two + back_through(
        grad_up_values, [half[1] for half in gate_up_w]
    )
    grad_gain_mlp = jnp.sum(grad_normed_two * normed_two, axis=0)
    scaled_two = grad_normed_two * gain_mlp
    grad_middle = grad_result.astype(jnp.float32) + inverse_two * (
        scaled_two - normed_two * jnp.mean(scaled_two * normed_two, axis=-1, keepdims=True)
    )
    grad_branch = grad_middle.astype(jnp.bfloat16)
    attended_gradient = back_through(grad_branch, out_rows).astype(jnp.bfloat16)
    delta_rows = jnp.sum(
        (attended_gradient.astype(jnp.float32) * mixture).reshape(
            device_rows, KEY_VALUE_HEADS, query_per_group, HEAD_WIDTH
        ),
        axis=-1,
    )
    delta_rows = delta_rows.transpose(1, 2, 0).reshape(KEY_VALUE_HEADS, 1, -1)
    key_value_terms, grad_query_lanes = attend_backward(
        bases,
        query_pos,
        key_value_all,
        queries,
        spread_heads(attended_gradient, KEY_VALUE_HEADS),
        log_total,
        delta_rows,
        half_rows,
    )
    grad_query_turned = (
        join_heads(
            jnp.stack(
                [
                    grad_query_lanes[g, g % 2 * HEAD_WIDTH : (g % 2 + 1) * HEAD_WIDTH]
                    for g in range(KEY_VALUE_HEADS)
                ]
            ),
            device_rows,
        )
        * scale_factor
    )
    key_value_gradient = jnp.concatenate(
        [
            scatter_keys(key_value_terms[: chunk_count // 2 * half_rows], "z", "y"),
            scatter_keys(key_value_terms[chunk_count // 2 * half_rows :], "y", "z"),
        ],
        axis=0,
    )
    grad_query_rows = (
        inverse_rotary(
            grad_query_turned.reshape(device_rows, QUERY_HEADS, HEAD_WIDTH),
            cosine_lookup,
            sine_lookup,
        )
        .reshape(device_rows, QUERY_HEADS * HEAD_WIDTH)
        .astype(jnp.bfloat16)
    )
    grad_query_out = scatter_halves(
        (grad_query_rows, grad_branch),
        list(zip(rounded_one, half_columns(attended, rows_w))),
        scatter_y_first,
    )
    grad_key_rows = (
        inverse_rotary(
            key_value_gradient[:, :width]
            .astype(jnp.float32)
            .reshape(device_rows, KEY_VALUE_HEADS, HEAD_WIDTH),
            cosine_lookup,
            sine_lookup,
        )
        .reshape(device_rows, width)
        .astype(jnp.bfloat16)
    )
    grad_value_rows = key_value_gradient[:, width:]
    grad_key_value = scatter_halves(
        (grad_key_rows, grad_value_rows), [(half, half) for half in rounded_one], scatter_y_first
    )
    grad_normed_one = back_through(grad_query_rows, [half[0] for half in query_out_w])
    grad_normed_one = grad_normed_one + back_through(
        grad_key_rows, [half[0] for half in key_value_w]
    )
    grad_normed_one = grad_normed_one + back_through(
        grad_value_rows, [half[1] for half in key_value_w]
    )
    grad_gain_attn = jnp.sum(grad_normed_one * normed_one, axis=0)
    scaled_one = grad_normed_one * gain_attn
    grad_inputs = grad_middle + inverse_one * (
        scaled_one - normed_one * jnp.mean(scaled_one * normed_one, axis=-1, keepdims=True)
    )

    def out(term):
        return term.astype(jnp.float32).T

    return (
        result[None],
        grad_inputs[None],
        total_sum(grad_gain_attn),
        out(grad_query_out[0]),
        out(grad_key_value[0]),
        out(grad_key_value[1]),
        out(grad_query_out[1]),
        total_sum(grad_gain_mlp),
        out(grad_gate_up[0]),
        out(grad_gate_up[1]),
        out(grad_down),
    )


def solution(mesh):
    grid = mesh.devices.reshape(4, 2, 4, 2, 2)
    fine = jax.sharding.Mesh(grid, AXES)
    rows = P(FSDP, CTX, None)
    weight = P(FSDP, CTX)
    return jax.shard_map(
        body,
        mesh=fine,
        in_specs=(
            rows,
            P(),
            P(),
            weight,
            weight,
            weight,
            weight,
            P(),
            weight,
            weight,
            weight,
            rows,
        ),
        out_specs=(
            rows,
            rows,
            P(),
            weight,
            weight,
            weight,
            weight,
            P(),
            weight,
            weight,
            weight,
        ),
        check_vma=False,
    )
```

```python
import functools
import math

import jax
import jax.numpy as jnp
from jax import lax
from jax.experimental import pallas as pl
from jax.experimental.pallas import tpu as pltpu
from jax.sharding import PartitionSpec as P

QUERY_HEADS = 15
KEY_VALUE_HEADS = 5
HEAD_WIDTH = 64


EPSILON = 1e-05
THETA = 10000.0
MASK_FLOOR = -1e30


def rope_tables(positions, head_size):
    half_size = head_size // 2
    frequencies = THETA ** (-2.0 * jnp.arange(half_size, dtype=jnp.float32) / head_size)
    angles = positions.astype(jnp.float32)[:, None] * frequencies[None, :]
    cosine = jnp.cos(angles)
    sine_part = jnp.sin(angles)
    cosine_lookup = jnp.concatenate([cosine, cosine], axis=1)[:, None, :]
    sine_lookup = jnp.concatenate([sine_part, sine_part], axis=1)[:, None, :]
    return (cosine_lookup, sine_lookup)


def apply_rotary(head_rows, cosine_lookup, sine_lookup):
    half_size = head_rows.shape[-1] // 2
    turned = jnp.concatenate([-head_rows[..., half_size:], head_rows[..., :half_size]], axis=-1)
    return head_rows * cosine_lookup + turned * sine_lookup


def inverse_rotary(grad_rows, cosine_lookup, sine_lookup):
    half_size = grad_rows.shape[-1] // 2
    moved = grad_rows * sine_lookup
    turned_back = jnp.concatenate([moved[..., half_size:], -moved[..., :half_size]], axis=-1)
    return grad_rows * cosine_lookup + turned_back


AXES = ("y", "xl", "z", "xh", "core")
CTX = ("y", "xl", "z")
FSDP = ("xh", "core")
RING = ("y", "z")
NEAR = ("xl", "xh", "core")
EXACT = lax.Precision.HIGHEST
COLUMN_SLOT = 32
SLOT_LANES = 256
UNIT_SLOT = 48
ATTN_ROWS = 64
MLP_ROWS = 3 * UNIT_SLOT


def shift(block, axis, step):
    size = lax.axis_size(axis)
    return lax.ppermute(block, axis, [(i, (i + step) % size) for i in range(size)])


def ring_gather(block, axis):
    ahead = shift(block, axis, -1)
    behind = shift(block, axis, 1)
    return [block, ahead, shift(block, axis, 2), behind]


def ring_sends(terms, axis):
    own, ahead, across, behind = terms
    return [own, shift(ahead, axis, 1), shift(behind, axis, -1), shift(across, axis, 2)]


def ring_sum(arrived):
    return add(*arrived)


def ring_scatter(terms, axis):
    return ring_sum(ring_sends(terms, axis))


def add(*terms):
    total = terms[0].astype(jnp.float32)
    for term in terms[1:]:
        total = total + term.astype(jnp.float32)
    return total.astype(jnp.bfloat16)


def pick(whole, axis, dim):
    index = lax.axis_index(axis)
    return [
        lax.dynamic_index_in_dim(whole, (index + j) % 4, dim, keepdims=False) for j in range(4)
    ]


def block_table(pair_table):
    y, xl, z = (lax.axis_index(axis) for axis in CTX)
    four = jnp.arange(4, dtype=jnp.int32)
    ys = ((y + four) % 4) * 8
    zs = (z + four) % 4
    xs = ((xl + jnp.arange(2, dtype=jnp.int32)) % 2) * 4
    low = ys[:, None, None] + zs[None, :, None] + xs[None, None, :]
    high = ys[None, :, None] + zs[:, None, None] + xs[None, None, :]
    count = pair_table.shape[0]

    def paired(owners):
        matches = owners.reshape(-1)[:, None] == jnp.arange(count, dtype=jnp.int32)[None, :]
        return jnp.sum(jnp.where(matches, pair_table[None, :], 0), axis=1, dtype=jnp.int32)

    return jnp.concatenate([paired(low), 2 * count - 1 - paired(high)])


def one_hot(source, size, valid=None):
    hits = jnp.arange(size, dtype=jnp.int32)[:, None] == source[None, :]
    if valid is not None:
        hits = hits & valid[None, :]
    return hits.astype(jnp.bfloat16)


def column_slots(columns):
    each = columns // 32
    slot = jnp.arange(32 * COLUMN_SLOT, dtype=jnp.int32)
    within = slot % COLUMN_SLOT
    owner = slot // COLUMN_SLOT
    owner = owner // 8 * 8 + owner % 2 * 4 + owner // 2 % 4
    return owner * each + within, within < each


def wide_place(column, part):
    return column // part * SLOT_LANES + column % part


def hidden_order(units):
    each = units // 32
    slot = jnp.arange(16 * UNIT_SLOT, dtype=jnp.int32)
    within = slot % UNIT_SLOT
    z = slot // UNIT_SLOT % 4
    fsdp = slot // (4 * UNIT_SLOT)
    place = ((within // each * 4 + z) * 4 + fsdp) * each + within % each
    return one_hot(place, units, within < 2 * each)


def key_value_order(columns, slot_rows):
    each = columns // 32
    slot = jnp.arange(32 * slot_rows, dtype=jnp.int32)
    within = slot % slot_rows
    owner = slot // slot_rows
    place = within // each * columns + owner * each + within % each
    return one_hot(place, 2 * columns, within < 2 * each)


def unpermute(values, order):
    return jnp.einsum(
        "ts,cs->tc",
        values,
        order.astype(jnp.float32),
        precision=EXACT,
        preferred_element_type=jnp.float32,
    )


def permute(values, order):
    return jnp.einsum("tc,cs->ts", values, order, preferred_element_type=jnp.float32).astype(
        jnp.bfloat16
    )


def forth(rows, weights):
    return jnp.einsum("td,ed->te", rows, weights, preferred_element_type=jnp.float32)


def back(grads, weights):
    return jnp.einsum("te,ed->td", grads, weights, preferred_element_type=jnp.float32)


def weight_term(left, right):
    return jnp.einsum("te,td->ed", left, right, preferred_element_type=jnp.float32).astype(
        jnp.bfloat16
    )


def pad_to(block, rows, lanes):
    return jnp.pad(block, ((0, rows - block.shape[0]), (0, lanes - block.shape[1])))


def exchange(chunks, axes):
    return lax.all_to_all(chunks, axes, 0, 0, tiled=True)


def widen(rows, part):
    count = rows.shape[0]
    rows = jnp.pad(rows.reshape(count, 4, part), ((0, 0), (0, 0), (0, SLOT_LANES - part)))
    return rows.reshape(count, 4 * SLOT_LANES)


def narrow(rows, part):
    count = rows.shape[0]
    return rows.reshape(count, 4, SLOT_LANES)[:, :, :part].reshape(count, 4 * part)


def lane_parts(rows):
    return [rows[..., i * SLOT_LANES : (i + 1) * SLOT_LANES] for i in range(rows.shape[-1] // SLOT_LANES)]


def core_halves(rows):
    parts = lane_parts(rows)
    even = jnp.concatenate([parts[0], parts[2]], axis=1)
    odd = jnp.concatenate([parts[1], parts[3]], axis=1)
    first = lax.axis_index("core") == 0
    return jnp.where(first, even, odd), jnp.where(first, odd, even)


def join_core_halves(own, other):
    first = lax.axis_index("core") == 0
    even = lane_parts(jnp.where(first, own, other))
    odd = lane_parts(jnp.where(first, other, own))
    return jnp.concatenate([even[0], odd[0], even[1], odd[1]], axis=1)


def from_four(rows):
    rows = jnp.concatenate([rows, shift(rows, "xh", 1)], axis=0)
    return jnp.concatenate([rows, shift(rows, "core", 1)], axis=0)


def to_four(partial):
    half = partial.shape[0] // 2
    partial = add(partial[:half], shift(partial[half:], "core", 1))
    half = half // 2
    return partial[:half].astype(jnp.float32) + shift(partial[half:], "xh", 1).astype(jnp.float32)


def fold_pieces():
    pieces = []
    for block in range(3):
        row = 0
        while row < 2 * COLUMN_SLOT:
            stacked = block * 2 * COLUMN_SLOT + row
            group, start = divmod(stacked, UNIT_SLOT)
            count = min(UNIT_SLOT - start, 2 * COLUMN_SLOT - row)
            pieces.append((row, count, block, start, group))
            row += count
    return pieces


def fold(rows):
    stacked = jnp.concatenate(lane_parts(rows), axis=0)
    return jnp.concatenate(
        [stacked[i * UNIT_SLOT : (i + 1) * UNIT_SLOT] for i in range(4)], axis=1
    )


def unfold(folded):
    stacked = jnp.concatenate(lane_parts(folded), axis=0)
    step = 2 * COLUMN_SLOT
    return jnp.concatenate([stacked[i * step : (i + 1) * step] for i in range(3)], axis=1)


def sum_from_all(terms):
    return jnp.sum(exchange(terms, AXES).astype(jnp.float32), axis=0)


def gain_rows(gain):
    gain = gain.reshape(4, SLOT_LANES)
    high = gain.astype(jnp.bfloat16)
    low = (gain - high.astype(jnp.float32)).astype(jnp.bfloat16)
    return jnp.broadcast_to(jnp.concatenate([high, low], axis=0)[None], (128, 8, SLOT_LANES))


def joined_gain(rows, part):
    return (rows[:4] + rows[4:])[:, :part].reshape(-1)


TILE = 512
LANES = 2 * HEAD_WIDTH


def lane_pair(part):
    return slice(part // 2 * LANES, part // 2 * LANES + LANES)


def fill_bias(base_ref, query_ref, bias_ref, half_rows):
    def step(chunk, carry):
        rows = pl.ds(chunk * half_rows, half_rows)
        position = base_ref[chunk] + lax.broadcasted_iota(jnp.int32, (half_rows, LANES), 0)
        bias_ref[rows, :] = jnp.where(position <= query_ref[...], 0.0, MASK_FLOOR)
        return carry

    lax.fori_loop(0, base_ref.shape[0], step, 0)


def tile_scores(kv_ref, rows, q_ref, bias, group):
    scores = lax.dot_general(
        kv_ref[rows, lane_pair(group)],
        q_ref[group],
        (((1,), (1,)), ((), ())),
        preferred_element_type=jnp.float32,
    )
    return scores + bias


def lay_pieces(piece_refs, kv_ref):
    rows = piece_refs[0].shape[0]
    for i, piece_ref in enumerate(piece_refs):
        kv_ref[i * rows : (i + 1) * rows, :] = piece_ref[...]


def attend_kernel(base_ref, query_ref, *refs, half_rows):
    *piece_refs, q_ref, o_ref, lse_ref, kv_ref, bias_ref = refs
    lay_pieces(piece_refs, kv_ref)
    fill_bias(base_ref, query_ref, bias_ref, half_rows)
    wide = q_ref.shape[1]
    tiles = kv_ref.shape[0] // TILE
    for group in range(KEY_VALUE_HEADS):

        def step(tile, carry, group=group):
            top, total, mixed = carry
            rows = pl.ds(pl.multiple_of(tile * TILE, TILE), TILE)
            bias = jnp.concatenate([bias_ref[rows, :]] * (wide // LANES), axis=1)
            scores = tile_scores(kv_ref, rows, q_ref, bias, group)
            new_top = jnp.maximum(top, jnp.max(scores, axis=0, keepdims=True))
            factor = jnp.exp(top - new_top)
            weights = jnp.exp(scores - new_top)
            total = total * factor + jnp.sum(weights, axis=0, keepdims=True)
            mixed = mixed * factor + lax.dot_general(
                kv_ref[rows, lane_pair(KEY_VALUE_HEADS + group)],
                weights.astype(jnp.bfloat16),
                (((0,), (0,)), ((), ())),
                preferred_element_type=jnp.float32,
            )
            return new_top, total, mixed

        top, total, mixed = lax.fori_loop(
            0,
            tiles,
            step,
            (
                jnp.full((1, wide), MASK_FLOOR, jnp.float32),
                jnp.zeros((1, wide), jnp.float32),
                jnp.zeros((LANES, wide), jnp.float32),
            ),
        )
        side = (KEY_VALUE_HEADS + group) % 2 * HEAD_WIDTH
        o_ref[group] = (mixed / total)[side : side + HEAD_WIDTH]
        lse_ref[group] = top + jnp.log(total)


def backward_kernel(base_ref, query_ref, *refs, half_rows):
    pieces = (len(refs) - 8) // 2
    piece_refs, refs = refs[:pieces], refs[pieces:]
    (q_ref, do_ref, lse_ref, delta_ref), refs = refs[:4], refs[4:]
    out_refs, (dq_ref, kv_ref, dkv_ref, bias_ref) = refs[:pieces], refs[pieces:]
    lay_pieces(piece_refs, kv_ref)
    fill_bias(base_ref, query_ref, bias_ref, half_rows)
    wide = q_ref.shape[1]
    tiles = kv_ref.shape[0] // TILE
    dq_ref[...] = jnp.zeros_like(dq_ref)

    def step(tile, carry):
        rows = pl.ds(pl.multiple_of(tile * TILE, TILE), TILE)
        bias = jnp.concatenate([bias_ref[rows, :]] * (wide // LANES), axis=1)
        sums = [None] * KEY_VALUE_HEADS

        def collect(part, term):
            pair = part // 2
            sums[pair] = term if sums[pair] is None else sums[pair] + term

        for group in range(KEY_VALUE_HEADS):
            scores = tile_scores(kv_ref, rows, q_ref, bias, group)
            probs = jnp.exp(scores - lse_ref[group])
            grad_probs = lax.dot_general(
                kv_ref[rows, lane_pair(KEY_VALUE_HEADS + group)],
                do_ref[group],
                (((1,), (1,)), ((), ())),
                preferred_element_type=jnp.float32,
            )
            ds = (probs * (grad_probs - delta_ref[group])).astype(jnp.bfloat16)
            collect(
                KEY_VALUE_HEADS + group,
                jnp.dot(
                    probs.astype(jnp.bfloat16), do_ref[group], preferred_element_type=jnp.float32
                ),
            )
            collect(group, jnp.dot(ds, q_ref[group], preferred_element_type=jnp.float32))
            dq_ref[group] += lax.dot_general(
                kv_ref[rows, lane_pair(group)],
                ds,
                (((0,), (0,)), ((), ())),
                preferred_element_type=jnp.float32,
            )
        for pair in range(KEY_VALUE_HEADS):
            dkv_ref[rows, pair * LANES : (pair + 1) * LANES] = sums[pair].astype(jnp.bfloat16)
        return carry

    lax.fori_loop(0, tiles, step, 0)
    for i, out_ref in enumerate(out_refs):
        out_ref[...] = dkv_ref[i * out_ref.shape[0] : (i + 1) * out_ref.shape[0], :]


def in_vmem():
    return pl.BlockSpec(memory_space=pltpu.VMEM)


def in_smem():
    return pl.BlockSpec(memory_space=pltpu.SMEM)


def spread_heads(rows, offset):
    count = rows.shape[0]
    heads = rows.reshape(count, KEY_VALUE_HEADS, -1, HEAD_WIDTH).transpose(1, 2, 0, 3)
    heads = heads.reshape(KEY_VALUE_HEADS, -1, HEAD_WIDTH)
    blank = jnp.zeros_like(heads)
    left = jnp.concatenate([heads, blank], axis=2)
    right = jnp.concatenate([blank, heads], axis=2)
    side = (offset + jnp.arange(KEY_VALUE_HEADS, dtype=jnp.int32)) % 2
    return jnp.where(side[:, None, None] == 0, left, right)


def join_heads(heads, count):
    heads = heads.reshape(KEY_VALUE_HEADS, HEAD_WIDTH, -1, count)
    return heads.transpose(3, 0, 2, 1).reshape(count, QUERY_HEADS * HEAD_WIDTH)


def attend(bases, query_pos, key_value, queries, half_rows):
    groups, wide, lanes = queries.shape
    keys, lanes_all = sum(piece.shape[0] for piece in key_value), key_value[0].shape[1]
    return pl.pallas_call(
        functools.partial(attend_kernel, half_rows=half_rows),
        out_shape=(
            jax.ShapeDtypeStruct((groups, HEAD_WIDTH, wide), jnp.float32),
            jax.ShapeDtypeStruct((groups, 1, wide), jnp.float32),
        ),
        in_specs=[in_smem()] + [in_vmem()] * (2 + len(key_value)),
        out_specs=(in_vmem(), in_vmem()),
        scratch_shapes=[
            pltpu.VMEM((keys, lanes_all), jnp.bfloat16),
            pltpu.VMEM((keys, lanes), jnp.float32),
        ],
        compiler_params=pltpu.CompilerParams(vmem_limit_bytes=40 * 2**20),
        cost_estimate=pl.CostEstimate(
            flops=4 * groups * wide * lanes * keys,
            bytes_accessed=keys * 640 * 2,
            transcendentals=groups * wide * keys,
        ),
        name="attend",
    )(bases, query_pos, *key_value, queries)


def attend_backward(bases, query_pos, key_value, queries, head_grads, lse, delta, half_rows):
    groups, wide, lanes = queries.shape
    keys, lanes_all = sum(piece.shape[0] for piece in key_value), key_value[0].shape[1]
    return pl.pallas_call(
        functools.partial(backward_kernel, half_rows=half_rows),
        out_shape=(
            *[jax.ShapeDtypeStruct(piece.shape, jnp.bfloat16) for piece in key_value],
            jax.ShapeDtypeStruct((groups, lanes, wide), jnp.float32),
        ),
        in_specs=[in_smem()] + [in_vmem()] * (5 + len(key_value)),
        out_specs=(in_vmem(),) * (len(key_value) + 1),
        scratch_shapes=[
            pltpu.VMEM((keys, lanes_all), jnp.bfloat16),
            pltpu.VMEM((keys, lanes_all), jnp.bfloat16),
            pltpu.VMEM((keys, lanes), jnp.float32),
        ],
        compiler_params=pltpu.CompilerParams(vmem_limit_bytes=40 * 2**20),
        cost_estimate=pl.CostEstimate(
            flops=10 * groups * wide * lanes * keys,
            bytes_accessed=keys * 640 * 4,
            transcendentals=groups * wide * keys,
        ),
        name="attend_backward",
    )(bases, query_pos, *key_value, queries, head_grads, lse, delta)


def dot_nt(left, right):
    return lax.dot_general(
        left, right, (((1,), (1,)), ((), ())), preferred_element_type=jnp.float32
    )


def dot_tn(left, right):
    return lax.dot_general(
        left, right, (((0,), (0,)), ((), ())), preferred_element_type=jnp.float32
    )


def mlp_kernel(
    w_ref, x_ref, dy_ref, down_ref, dx_ref, term_ref, wg_ref, wu_ref, wd_ref, h_ref, dg_ref, du_ref
):
    blocks = w_ref.shape[0]
    slots = 2 * COLUMN_SLOT

    def unpack(i, carry):
        units = pl.ds(pl.multiple_of(i * UNIT_SLOT, 16), UNIT_SLOT)
        wg_ref[units, :] = w_ref[i, :UNIT_SLOT]
        wu_ref[units, :] = w_ref[i, UNIT_SLOT : 2 * UNIT_SLOT]
        first = 2 * UNIT_SLOT
        for row, count, block, start, group in fold_pieces():
            wd_ref[
                pl.ds(pl.multiple_of(i * slots + row, 16), count),
                block * SLOT_LANES : (block + 1) * SLOT_LANES,
            ] = w_ref[
                i,
                first + start : first + start + count,
                group * SLOT_LANES : (group + 1) * SLOT_LANES,
            ]
        return carry

    lax.fori_loop(0, blocks, unpack, 0)
    step_rows = 256
    for step in range(x_ref.shape[0] // step_rows):
        rows = slice(step * step_rows, (step + 1) * step_rows)
        x = x_ref[rows]
        dy = dy_ref[rows]
        gate = dot_nt(x, wg_ref[...])
        up = dot_nt(x, wu_ref[...])
        sigmoid = jax.nn.sigmoid(gate)
        silu = gate * sigmoid
        hidden = (silu * up).astype(jnp.bfloat16)
        h_ref[rows] = hidden
        down_ref[rows] = dot_nt(hidden, wd_ref[...]).astype(jnp.bfloat16)
        dh = jnp.dot(dy, wd_ref[...], preferred_element_type=jnp.float32)
        dgate = (dh * up * sigmoid * (1.0 + gate * (1.0 - sigmoid))).astype(jnp.bfloat16)
        dup = (dh * silu).astype(jnp.bfloat16)
        dg_ref[rows] = dgate
        du_ref[rows] = dup
        dx = jnp.dot(dgate, wg_ref[...], preferred_element_type=jnp.float32)
        dx = dx + jnp.dot(dup, wu_ref[...], preferred_element_type=jnp.float32)
        dx_ref[rows] = dx.astype(jnp.bfloat16)
    per = 8
    for part in range(blocks // per):
        lanes = slice(part * per * UNIT_SLOT, (part + 1) * per * UNIT_SLOT)
        for at, grads in ((0, dg_ref), (UNIT_SLOT, du_ref)):
            term = dot_tn(grads[:, lanes], x_ref[...]).astype(jnp.bfloat16)
            for i in range(per):
                term_ref[part * per + i, at : at + UNIT_SLOT] = term[
                    i * UNIT_SLOT : (i + 1) * UNIT_SLOT
                ]
    per = 4
    for part in range(blocks // per):
        lanes = slice(part * per * slots, (part + 1) * per * slots)
        term = dot_tn(dy_ref[:, lanes], h_ref[...]).astype(jnp.bfloat16)
        for i in range(per):
            for row, count, block, start, group in fold_pieces():
                term_ref[
                    part * per + i,
                    2 * UNIT_SLOT + start : 2 * UNIT_SLOT + start + count,
                    group * SLOT_LANES : (group + 1) * SLOT_LANES,
                ] = term[
                    i * slots + row : i * slots + row + count,
                    block * SLOT_LANES : (block + 1) * SLOT_LANES,
                ]


def query_kernel(
    lanes_ref,
    cos_ref,
    sin_ref,
    order_ref,
    branch_ref,
    h_own_ref,
    h_other_ref,
    a_own_ref,
    a_other_ref,
    w_own_ref,
    w_other_ref,
    own_ref,
    other_ref,
    back_ref,
    dq_ref,
    *,
    scale_factor,
):
    half = HEAD_WIDTH // 2
    cos = cos_ref[...]
    sin = sin_ref[...]
    tokens = cos.shape[1]
    heads = lanes_ref.shape[2] // tokens
    for group in range(KEY_VALUE_HEADS):
        at = group % 2 * HEAD_WIDTH
        for head in range(heads):
            lanes = slice(head * tokens, (head + 1) * tokens)
            top = lanes_ref[group, at : at + half, lanes] * scale_factor
            low = lanes_ref[group, at + half : at + HEAD_WIDTH, lanes] * scale_factor
            row = (group * heads + head) * HEAD_WIDTH
            dq_ref[row : row + half] = (top * cos + low * sin).astype(jnp.bfloat16)
            dq_ref[row + half : row + HEAD_WIDTH] = (low * cos - top * sin).astype(jnp.bfloat16)
    slots = dot_tn(order_ref[...], dq_ref[...]).astype(jnp.bfloat16)
    cut = h_own_ref.shape[1]
    sides = (
        (own_ref, h_own_ref, a_own_ref, w_own_ref),
        (other_ref, h_other_ref, a_other_ref, w_other_ref),
    )
    for i, (out_ref, h_ref, a_ref, w_ref) in enumerate(sides):
        out_ref[:, :cut] = jnp.dot(
            slots, h_ref[...], preferred_element_type=jnp.float32
        ).astype(jnp.bfloat16)
        out_ref[:, cut:] = dot_tn(branch_ref[...], a_ref[...]).astype(jnp.bfloat16)
        back_ref[i] = dot_tn(slots, w_ref[:, :cut])


def query_terms(grad_lanes, cosine, sine, order, branch, rows, mixed, weights, scale_factor):
    columns, slots = order.shape
    count, cut = rows[0].shape
    return pl.pallas_call(
        functools.partial(query_kernel, scale_factor=scale_factor),
        out_shape=(
            jax.ShapeDtypeStruct((slots, 2 * cut), jnp.bfloat16),
            jax.ShapeDtypeStruct((slots, 2 * cut), jnp.bfloat16),
            jax.ShapeDtypeStruct((2, count, cut), jnp.float32),
        ),
        in_specs=[in_vmem()] * 11,
        out_specs=(in_vmem(),) * 3,
        scratch_shapes=[pltpu.VMEM((columns, count), jnp.bfloat16)],
        compiler_params=pltpu.CompilerParams(vmem_limit_bytes=40 * 2**20),
        cost_estimate=pl.CostEstimate(
            flops=2 * 10**10, bytes_accessed=4 * 10**7, transcendentals=0
        ),
        name="query_terms",
    )(grad_lanes, cosine, sine, order, branch, *rows, *mixed, *weights)


def feed_forward(weights, rows, grads):
    blocks = weights.shape[0]
    count, wide = rows.shape
    units = blocks * UNIT_SLOT
    slots = blocks * 2 * COLUMN_SLOT
    return pl.pallas_call(
        mlp_kernel,
        out_shape=(
            jax.ShapeDtypeStruct((count, slots), jnp.bfloat16),
            jax.ShapeDtypeStruct((count, wide), jnp.bfloat16),
            jax.ShapeDtypeStruct((blocks, MLP_ROWS, wide), jnp.bfloat16),
        ),
        in_specs=[in_vmem()] * 3,
        out_specs=(in_vmem(),) * 3,
        scratch_shapes=[
            pltpu.VMEM((units, wide), jnp.bfloat16),
            pltpu.VMEM((units, wide), jnp.bfloat16),
            pltpu.VMEM((slots, units), jnp.bfloat16),
            pltpu.VMEM((count, units), jnp.bfloat16),
            pltpu.VMEM((count, units), jnp.bfloat16),
            pltpu.VMEM((count, units), jnp.bfloat16),
        ],
        compiler_params=pltpu.CompilerParams(vmem_limit_bytes=48 * 2**20),
        cost_estimate=pl.CostEstimate(
            flops=18 * count * units * wide,
            bytes_accessed=2 * weights.size * 2,
            transcendentals=count * units,
        ),
        name="feed_forward",
    )(weights, rows, grads)


def body(
    tokens,
    pair_table,
    gain_attn,
    w_query,
    w_key,
    w_value,
    w_out,
    gain_mlp,
    w_gate,
    w_up,
    w_down,
    cotangent,
):
    device_rows, columns = tokens.shape[1:]
    half_rows = device_rows // 2
    width = HEAD_WIDTH * KEY_VALUE_HEADS
    query_per_group = QUERY_HEADS // KEY_VALUE_HEADS
    scale_factor = 1.0 / math.sqrt(HEAD_WIDTH)
    part, each = w_query.shape
    each_key = w_key.shape[1]
    each_unit = w_gate.shape[1] // 4
    unit_rows = -(-each_unit // 8) * 8
    unit_lanes = 4 * UNIT_SLOT
    slot = COLUMN_SLOT
    first_core = lax.axis_index("core") == 0
    within = jnp.arange(half_rows, dtype=jnp.int32)
    blocks = block_table(pair_table)
    chunk_count = blocks.shape[0]
    own_pos = jnp.concatenate(
        [blocks[0] * half_rows + within, blocks[chunk_count // 2] * half_rows + within]
    )
    cosine_lookup, sine_lookup = rope_tables(own_pos, HEAD_WIDTH)
    slot_column, slot_used = column_slots(columns)
    head_order = one_hot(slot_column, columns, slot_used)
    order = one_hot(wide_place(slot_column, part), 4 * SLOT_LANES, slot_used)
    unit_order = hidden_order(w_down.shape[0])
    key_rows = -(-2 * each_key // 8) * 8
    key_order = key_value_order(width, key_rows)

    key_chunk = pad_to(jnp.concatenate([w_key.T, w_value.T], axis=0), key_rows, SLOT_LANES)
    key_all = exchange(jnp.broadcast_to(key_chunk[None], (128,) + key_chunk.shape), AXES)

    down_units = jnp.einsum(
        "fd,fu->du", w_down, unit_order, preferred_element_type=jnp.float32
    ).astype(jnp.bfloat16)
    shared = [pad_to(w_query.T, slot, SLOT_LANES), pad_to(w_out.T, slot, SLOT_LANES)]

    def for_fsdp(fsdp):
        units = slice(fsdp * each_unit, (fsdp + 1) * each_unit)
        return jnp.concatenate(
            shared
            + [
                pad_to(w_gate.T[units], unit_rows, SLOT_LANES),
                pad_to(w_up.T[units], unit_rows, SLOT_LANES),
                pad_to(
                    down_units[:, fsdp * unit_lanes : (fsdp + 1) * unit_lanes], slot, SLOT_LANES
                ),
            ],
            axis=0,
        )

    chunk = jnp.stack([for_fsdp(i) for i in range(4)])
    chunk, key_all = lax.optimization_barrier((chunk, key_all))
    near = exchange(jnp.concatenate([chunk, chunk], axis=0), NEAR)
    near = near.reshape((2, 4) + near.shape[1:])
    mine = jnp.where(first_core, near[:, 0::2, : 2 * slot], near[:, 1::2, : 2 * slot])
    shard_attn = jnp.concatenate(
        [mine[:, i, j * slot : (j + 1) * slot] for j in range(2) for i in range(2)], axis=2
    ).reshape(2 * slot, 4 * SLOT_LANES)

    def lay_units(start):
        cut = near[:, :, start : start + each_unit]
        rows = [jnp.concatenate([cut[x, i] for i in range(4)], axis=1) for x in range(2)]
        return pad_to(jnp.concatenate(rows, axis=0), UNIT_SLOT, 4 * SLOT_LANES)

    shard_down = near[:, :, 2 * slot + 2 * unit_rows :, :unit_lanes]
    shard_down = jnp.concatenate([shard_down[:, i] for i in range(4)], axis=2)
    attn_own = lax.all_gather(shard_attn[None], RING, axis=0, tiled=True)
    attn_own = attn_own.reshape(-1, 4 * SLOT_LANES)
    packed = jnp.concatenate(
        [
            lay_units(2 * slot),
            lay_units(2 * slot + unit_rows),
            fold(shard_down.reshape(2 * slot, 4 * unit_lanes)),
        ],
        axis=0,
    )
    def forth_halves(rows, halves):
        own, other = core_halves(rows)
        return forth(own, halves[0]) + forth(other, halves[1])

    def back_halves(grads, halves):
        return join_core_halves(back(grads, halves[0]), back(grads, halves[1]))

    key_all = key_all.reshape(32, 4, key_rows, SLOT_LANES)
    key_value_w = [key_all[:, i].reshape(-1, SLOT_LANES) for i in range(4)]

    def mean_of(rows):
        return jnp.sum(rows, axis=-1, keepdims=True) / columns

    wide_gain_attn = widen(gain_attn[None], part)
    wide_gain_mlp = widen(gain_mlp[None], part)
    inputs = widen(tokens[0].astype(jnp.float32), part)
    inverse_one = lax.rsqrt(mean_of(inputs * inputs) + EPSILON)
    normed_one = inputs * inverse_one
    rounded_one = (normed_one * wide_gain_attn).astype(jnp.bfloat16)
    key_value_raw = sum(
        forth(rows, weights) for rows, weights in zip(lane_parts(rounded_one), key_value_w)
    )
    key_value_raw = unpermute(key_value_raw, key_order)
    key_local = (
        apply_rotary(
            key_value_raw[:, :width].reshape(device_rows, KEY_VALUE_HEADS, HEAD_WIDTH),
            cosine_lookup,
            sine_lookup,
        )
        .astype(jnp.bfloat16)
        .reshape(device_rows, width)
    )
    key_value = jnp.concatenate([key_local, key_value_raw[:, width:].astype(jnp.bfloat16)], axis=1)
    other = shift(key_value, "xl", 1)
    low_rows = jnp.concatenate([key_value[:half_rows], other[:half_rows]], axis=0)
    high_rows = jnp.concatenate([key_value[half_rows:], other[half_rows:]], axis=0)
    low_rows = jnp.concatenate(ring_gather(low_rows, "z"), axis=0)
    high_rows = jnp.concatenate(ring_gather(high_rows, "y"), axis=0)
    grad_result = widen(cotangent[0], part)
    grad_slots = from_four(permute(grad_result, order))
    low_rows, high_rows, grad_slots = lax.optimization_barrier((low_rows, high_rows, grad_slots))
    key_value_all = ring_gather(low_rows, "y") + ring_gather(high_rows, "z")
    key_value_all, attn_own, packed = lax.optimization_barrier((key_value_all, attn_own, packed))
    packed = lax.all_gather(packed[None], RING, axis=0, tiled=True)
    attn_w = (attn_own, shift(attn_own, "core", 1))
    query_w = [half[:, : 2 * SLOT_LANES] for half in attn_w]
    out_w = [half[:, 2 * SLOT_LANES :] for half in attn_w]
    query_raw = unpermute(forth_halves(rounded_one, query_w), head_order).reshape(
        device_rows, QUERY_HEADS, HEAD_WIDTH
    )
    query_heads = apply_rotary(query_raw, cosine_lookup, sine_lookup).astype(jnp.bfloat16)
    queries = spread_heads(
        query_heads.reshape(device_rows, QUERY_HEADS * HEAD_WIDTH)
        * jnp.asarray(scale_factor, jnp.bfloat16),
        0,
    )
    bases = blocks * half_rows
    query_pos = own_pos[None, :]
    mixed, log_total = attend(bases, query_pos, key_value_all, queries, half_rows)
    mixture = join_heads(mixed, device_rows)
    attended = mixture.astype(jnp.bfloat16)
    wide_attended = widen(attended, part)
    middle = inputs + unpermute(forth_halves(wide_attended, out_w), order)
    inverse_two = lax.rsqrt(mean_of(middle * middle) + EPSILON)
    normed_two = middle * inverse_two
    rounded_two = (normed_two * wide_gain_mlp).astype(jnp.bfloat16)
    down_sums, unit_sums, ring_terms = feed_forward(
        packed, from_four(rounded_two), grad_slots
    )
    sums = to_four(jnp.concatenate([unit_sums, down_sums], axis=1))
    grad_normed_two = sums[:, : 4 * SLOT_LANES]
    down_sums = sums[:, 4 * SLOT_LANES :]
    ring_terms = lax.psum_scatter(ring_terms, "y", scatter_dimension=0, tiled=True)
    grad_gain_mlp = jnp.sum(grad_normed_two * normed_two, axis=0)
    scaled_two = grad_normed_two * wide_gain_mlp
    grad_middle = grad_result.astype(jnp.float32) + inverse_two * (
        scaled_two - normed_two * mean_of(scaled_two * normed_two)
    )
    grad_branch = permute(grad_middle.astype(jnp.bfloat16), order)
    attended_gradient = narrow(back_halves(grad_branch, out_w).astype(jnp.bfloat16), part)
    delta_rows = jnp.sum(
        (attended_gradient.astype(jnp.float32) * mixture).reshape(
            device_rows, KEY_VALUE_HEADS, query_per_group, HEAD_WIDTH
        ),
        axis=-1,
    )
    delta_rows = delta_rows.transpose(1, 2, 0).reshape(KEY_VALUE_HEADS, 1, -1)
    *key_value_terms, grad_query_lanes = attend_backward(
        bases,
        query_pos,
        key_value_all,
        queries,
        spread_heads(attended_gradient, KEY_VALUE_HEADS),
        log_total,
        delta_rows,
        half_rows,
    )
    key_value_terms, ring_terms = lax.optimization_barrier((key_value_terms, ring_terms))
    low_arrived = ring_sends(key_value_terms[:4], "y")
    high_arrived = ring_sends(key_value_terms[4:], "z")
    low_arrived, high_arrived = lax.optimization_barrier((low_arrived, high_arrived))

    *attn_terms, query_back = query_terms(
        grad_query_lanes,
        cosine_lookup[:, 0, : HEAD_WIDTH // 2].T,
        sine_lookup[:, 0, : HEAD_WIDTH // 2].T,
        head_order,
        grad_branch,
        core_halves(rounded_one),
        core_halves(wide_attended),
        attn_w,
        scale_factor,
    )
    attn_terms = add(attn_terms[0], shift(attn_terms[1], "core", 1))
    attn_terms = lax.psum_scatter(
        attn_terms.reshape(16, ATTN_ROWS, -1), "y", scatter_dimension=0, tiled=True
    )
    key_value_near = jnp.concatenate(
        [
            ring_scatter(jnp.split(ring_sum(low_arrived), 4, axis=0), "z"),
            ring_scatter(jnp.split(ring_sum(high_arrived), 4, axis=0), "y"),
        ],
        axis=0,
    )
    key_value_near, attn_terms, ring_terms = lax.optimization_barrier(
        (key_value_near, attn_terms, ring_terms)
    )
    key_value_near = key_value_near.reshape(2, 2, half_rows, 2 * width)
    key_value_gradient = add(
        key_value_near[:, 0].reshape(device_rows, -1),
        shift(key_value_near[:, 1].reshape(device_rows, -1), "xl", 1),
    )
    key_value_gradient, down_sums = lax.optimization_barrier((key_value_gradient, down_sums))
    result = (middle + unpermute(down_sums, order)).astype(jnp.bfloat16)
    grad_key_rows = (
        inverse_rotary(
            key_value_gradient[:, :width]
            .astype(jnp.float32)
            .reshape(device_rows, KEY_VALUE_HEADS, HEAD_WIDTH),
            cosine_lookup,
            sine_lookup,
        )
        .reshape(device_rows, width)
        .astype(jnp.bfloat16)
    )
    grad_key_slots = permute(
        jnp.concatenate([grad_key_rows, key_value_gradient[:, width:]], axis=1), key_order
    )
    grad_normed_one = join_core_halves(query_back[0], query_back[1]) + jnp.concatenate(
        [back(grad_key_slots, weights) for weights in key_value_w], axis=1
    )
    scaled_one = grad_normed_one * wide_gain_attn
    grad_inputs = grad_middle + inverse_one * (
        scaled_one - normed_one * mean_of(scaled_one * normed_one)
    )

    key_terms = jnp.stack(
        [
            weight_term(grad_key_slots, rows).reshape(32, key_rows, SLOT_LANES)
            for rows in lane_parts(rounded_one)
        ],
        axis=1,
    ).reshape(128, key_rows, SLOT_LANES)
    gain_terms = gain_rows(jnp.sum(grad_normed_one * normed_one, axis=0))
    key_terms = jnp.concatenate([key_terms, gain_terms, gain_rows(grad_gain_mlp)], axis=1)
    ring_terms = jnp.concatenate([attn_terms, ring_terms], axis=1)
    ring_terms = ring_scatter(pick(ring_terms, "z", 0), "z")
    gate_at = ATTN_ROWS
    up_at = gate_at + UNIT_SLOT
    down_terms = unfold(ring_terms[up_at + UNIT_SLOT :])

    def chunk_for(xl, fsdp):
        lanes = slice(fsdp * SLOT_LANES, (fsdp + 1) * SLOT_LANES)
        at = fsdp // 2 * SLOT_LANES
        query_lanes = slice(at, at + SLOT_LANES)
        out_lanes = slice(2 * SLOT_LANES + at, 3 * SLOT_LANES + at)
        slots = slice(xl * slot, (xl + 1) * slot)
        units = xl * each_unit
        return jnp.concatenate(
            [
                ring_terms[slots, query_lanes],
                ring_terms[slots, out_lanes],
                pad_to(
                    ring_terms[gate_at + units : gate_at + units + each_unit, lanes],
                    unit_rows,
                    SLOT_LANES,
                ),
                pad_to(
                    ring_terms[up_at + units : up_at + units + each_unit, lanes],
                    unit_rows,
                    SLOT_LANES,
                ),
                pad_to(
                    down_terms[slots, fsdp * unit_lanes : (fsdp + 1) * unit_lanes],
                    slot,
                    SLOT_LANES,
                ),
            ],
            axis=0,
        )

    chunks = jnp.stack([chunk_for(xl, fsdp) for xl in range(2) for fsdp in range(4)])
    key_sums = exchange(key_terms, AXES)
    chunks, key_sums = lax.optimization_barrier((chunks, key_sums))
    near = exchange(chunks, NEAR).astype(jnp.float32)
    key_sums = jnp.sum(key_sums.astype(jnp.float32), axis=0)
    near = near.reshape((2, 4) + near.shape[1:]).sum(axis=0)
    attn_sums = near[:, : 2 * slot]
    attn_sums = jnp.where(
        first_core, attn_sums[0] + attn_sums[2], attn_sums[1] + attn_sums[3]
    )
    grad_query = attn_sums[:each, :part]
    grad_out = attn_sums[slot : slot + each, :part]
    at = 2 * slot
    grad_gate = near[:, at : at + each_unit, :part].reshape(-1, part)
    at = at + unit_rows
    grad_up = near[:, at : at + each_unit, :part].reshape(-1, part)
    at = at + unit_rows
    grad_down = jnp.concatenate([near[i, at:, :unit_lanes] for i in range(4)], axis=1)
    grad_down = jnp.einsum(
        "du,fu->fd",
        grad_down,
        unit_order.astype(jnp.float32),
        precision=EXACT,
        preferred_element_type=jnp.float32,
    )

    grad_key = key_sums[:each_key, :part]
    grad_value = key_sums[each_key : 2 * each_key, :part]
    grad_gain_attn = joined_gain(key_sums[key_rows : key_rows + 8], part)
    grad_gain_mlp = joined_gain(key_sums[key_rows + 8 :], part)

    return (
        narrow(result, part)[None],
        narrow(grad_inputs, part)[None],
        grad_gain_attn,
        grad_query.T,
        grad_key.T,
        grad_value.T,
        grad_out.T,
        grad_gain_mlp,
        grad_gate.T,
        grad_up.T,
        grad_down[:, :each],
    )


def solution(mesh):
    grid = mesh.devices.reshape(4, 2, 4, 2, 2)
    fine = jax.sharding.Mesh(grid, AXES)
    rows = P(FSDP, CTX, None)
    weight = P(FSDP, CTX)
    return jax.shard_map(
        body,
        mesh=fine,
        in_specs=(
            rows,
            P(),
            P(),
            weight,
            weight,
            weight,
            weight,
            P(),
            weight,
            weight,
            weight,
            rows,
        ),
        out_specs=(
            rows,
            rows,
            P(),
            weight,
            weight,
            weight,
            weight,
            P(),
            weight,
            weight,
            weight,
        ),
        check_vma=False,
    )
```

```python
import functools
import math

import jax
import jax.numpy as jnp
from jax import lax
from jax.experimental import pallas as pl
from jax.experimental.pallas import tpu as pltpu
from jax.sharding import PartitionSpec as P

QUERY_HEADS = 15
KEY_VALUE_HEADS = 5
HEAD_WIDTH = 64


EPSILON = 1e-05
THETA = 10000.0
MASK_FLOOR = -1e30


def rope_tables(positions, head_size):
    half_size = head_size // 2
    frequencies = THETA ** (-2.0 * jnp.arange(half_size, dtype=jnp.float32) / head_size)
    angles = positions.astype(jnp.float32)[:, None] * frequencies[None, :]
    cosine = jnp.cos(angles)
    sine_part = jnp.sin(angles)
    cosine_lookup = jnp.concatenate([cosine, cosine], axis=1)[:, None, :]
    sine_lookup = jnp.concatenate([sine_part, sine_part], axis=1)[:, None, :]
    return (cosine_lookup, sine_lookup)


def apply_rotary(head_rows, cosine_lookup, sine_lookup):
    half_size = head_rows.shape[-1] // 2
    turned = jnp.concatenate([-head_rows[..., half_size:], head_rows[..., :half_size]], axis=-1)
    return head_rows * cosine_lookup + turned * sine_lookup


def inverse_rotary(grad_rows, cosine_lookup, sine_lookup):
    half_size = grad_rows.shape[-1] // 2
    moved = grad_rows * sine_lookup
    turned_back = jnp.concatenate([moved[..., half_size:], -moved[..., :half_size]], axis=-1)
    return grad_rows * cosine_lookup + turned_back


AXES = ("y", "xl", "z", "xh", "core")
CTX = ("y", "xl", "z")
FSDP = ("xh", "core")
RING = ("y", "z")
NEAR = ("xl", "xh", "core")
EXACT = lax.Precision.HIGHEST
COLUMN_SLOT = 32
SLOT_LANES = 256
UNIT_SLOT = 48
ATTN_ROWS = 64
MLP_ROWS = 3 * UNIT_SLOT


def shift(block, axis, step):
    size = lax.axis_size(axis)
    return lax.ppermute(block, axis, [(i, (i + step) % size) for i in range(size)])


def ring_gather(block, axis):
    ahead = shift(block, axis, -1)
    behind = shift(block, axis, 1)
    return [block, ahead, shift(block, axis, 2), behind]


def ring_sends(terms, axis):
    own, ahead, across, behind = terms
    return [own, shift(ahead, axis, 1), shift(behind, axis, -1), shift(across, axis, 2)]


def ring_sum(arrived):
    return add(*arrived)


def ring_scatter(terms, axis):
    return ring_sum(ring_sends(terms, axis))


def add(*terms):
    total = terms[0].astype(jnp.float32)
    for term in terms[1:]:
        total = total + term.astype(jnp.float32)
    return total.astype(jnp.bfloat16)


def pick(whole, axis, dim):
    index = lax.axis_index(axis)
    return [
        lax.dynamic_index_in_dim(whole, (index + j) % 4, dim, keepdims=False) for j in range(4)
    ]


def block_table(pair_table):
    y, xl, z = (lax.axis_index(axis) for axis in CTX)
    four = jnp.arange(4, dtype=jnp.int32)
    ys = ((y + four) % 4) * 8
    zs = (z + four) % 4
    xs = ((xl + jnp.arange(2, dtype=jnp.int32)) % 2) * 4
    low = ys[:, None, None] + zs[None, :, None] + xs[None, None, :]
    high = ys[None, :, None] + zs[:, None, None] + xs[None, None, :]
    count = pair_table.shape[0]

    def paired(owners):
        matches = owners.reshape(-1)[:, None] == jnp.arange(count, dtype=jnp.int32)[None, :]
        return jnp.sum(jnp.where(matches, pair_table[None, :], 0), axis=1, dtype=jnp.int32)

    return jnp.concatenate([paired(low), 2 * count - 1 - paired(high)])


def one_hot(source, size, valid=None):
    hits = jnp.arange(size, dtype=jnp.int32)[:, None] == source[None, :]
    if valid is not None:
        hits = hits & valid[None, :]
    return hits.astype(jnp.bfloat16)


def column_slots(columns):
    each = columns // 32
    slot = jnp.arange(32 * COLUMN_SLOT, dtype=jnp.int32)
    within = slot % COLUMN_SLOT
    owner = slot // COLUMN_SLOT
    owner = owner // 8 * 8 + owner % 2 * 4 + owner // 2 % 4
    return owner * each + within, within < each


def wide_place(column, part):
    return column // part * SLOT_LANES + column % part


def hidden_order(units):
    each = units // 32
    slot = jnp.arange(16 * UNIT_SLOT, dtype=jnp.int32)
    within = slot % UNIT_SLOT
    z = slot // UNIT_SLOT % 4
    fsdp = slot // (4 * UNIT_SLOT)
    place = ((within // each * 4 + z) * 4 + fsdp) * each + within % each
    return one_hot(place, units, within < 2 * each)


def key_value_order(columns, slot_rows):
    each = columns // 32
    slot = jnp.arange(32 * slot_rows, dtype=jnp.int32)
    within = slot % slot_rows
    owner = slot // slot_rows
    place = within // each * columns + owner * each + within % each
    return one_hot(place, 2 * columns, within < 2 * each)


def unpermute(values, order):
    return jnp.einsum(
        "ts,cs->tc",
        values,
        order.astype(jnp.float32),
        precision=EXACT,
        preferred_element_type=jnp.float32,
    )


def permute(values, order):
    return jnp.einsum("tc,cs->ts", values, order, preferred_element_type=jnp.float32).astype(
        jnp.bfloat16
    )


def forth(rows, weights):
    return jnp.einsum("td,ed->te", rows, weights, preferred_element_type=jnp.float32)


def back(grads, weights):
    return jnp.einsum("te,ed->td", grads, weights, preferred_element_type=jnp.float32)


def weight_term(left, right):
    return jnp.einsum("te,td->ed", left, right, preferred_element_type=jnp.float32).astype(
        jnp.bfloat16
    )


def pad_to(block, rows, lanes):
    return jnp.pad(block, ((0, rows - block.shape[0]), (0, lanes - block.shape[1])))


def exchange(chunks, axes):
    return lax.all_to_all(chunks, axes, 0, 0, tiled=True)


def widen(rows, part):
    count = rows.shape[0]
    rows = jnp.pad(rows.reshape(count, 4, part), ((0, 0), (0, 0), (0, SLOT_LANES - part)))
    return rows.reshape(count, 4 * SLOT_LANES)


def narrow(rows, part):
    count = rows.shape[0]
    return rows.reshape(count, 4, SLOT_LANES)[:, :, :part].reshape(count, 4 * part)


def lane_parts(rows):
    return [rows[..., i * SLOT_LANES : (i + 1) * SLOT_LANES] for i in range(rows.shape[-1] // SLOT_LANES)]


def core_halves(rows):
    parts = lane_parts(rows)
    even = jnp.concatenate([parts[0], parts[2]], axis=1)
    odd = jnp.concatenate([parts[1], parts[3]], axis=1)
    first = lax.axis_index("core") == 0
    return jnp.where(first, even, odd), jnp.where(first, odd, even)


def join_core_halves(own, other):
    first = lax.axis_index("core") == 0
    even = lane_parts(jnp.where(first, own, other))
    odd = lane_parts(jnp.where(first, other, own))
    return jnp.concatenate([even[0], odd[0], even[1], odd[1]], axis=1)


def from_four(rows):
    rows = jnp.concatenate([rows, shift(rows, "xh", 1)], axis=0)
    return jnp.concatenate([rows, shift(rows, "core", 1)], axis=0)


def to_four(partial):
    half = partial.shape[0] // 2
    partial = add(partial[:half], shift(partial[half:], "core", 1))
    half = half // 2
    return partial[:half].astype(jnp.float32) + shift(partial[half:], "xh", 1).astype(jnp.float32)


def fold_pieces():
    pieces = []
    for block in range(3):
        row = 0
        while row < 2 * COLUMN_SLOT:
            stacked = block * 2 * COLUMN_SLOT + row
            group, start = divmod(stacked, UNIT_SLOT)
            count = min(UNIT_SLOT - start, 2 * COLUMN_SLOT - row)
            pieces.append((row, count, block, start, group))
            row += count
    return pieces


def fold(rows):
    stacked = jnp.concatenate(lane_parts(rows), axis=0)
    return jnp.concatenate(
        [stacked[i * UNIT_SLOT : (i + 1) * UNIT_SLOT] for i in range(4)], axis=1
    )


def unfold(folded):
    stacked = jnp.concatenate(lane_parts(folded), axis=0)
    step = 2 * COLUMN_SLOT
    return jnp.concatenate([stacked[i * step : (i + 1) * step] for i in range(3)], axis=1)


def sum_from_all(terms):
    return jnp.sum(exchange(terms, AXES).astype(jnp.float32), axis=0)


def gain_rows(gain):
    gain = gain.reshape(4, SLOT_LANES)
    high = gain.astype(jnp.bfloat16)
    low = (gain - high.astype(jnp.float32)).astype(jnp.bfloat16)
    return jnp.broadcast_to(jnp.concatenate([high, low], axis=0)[None], (128, 8, SLOT_LANES))


def joined_gain(rows, part):
    return (rows[:4] + rows[4:])[:, :part].reshape(-1)


TILE = 1024
LANES = 2 * HEAD_WIDTH


def lane_pair(part):
    return slice(part // 2 * LANES, part // 2 * LANES + LANES)


def fill_bias(base_ref, query_ref, bias_ref, half_rows):
    def step(chunk, carry):
        rows = pl.ds(chunk * half_rows, half_rows)
        position = base_ref[chunk] + lax.broadcasted_iota(jnp.int32, (half_rows, LANES), 0)
        bias_ref[rows, :] = jnp.where(position <= query_ref[...], 0.0, MASK_FLOOR)
        return carry

    lax.fori_loop(0, base_ref.shape[0], step, 0)


def tile_scores(kv_ref, rows, q_ref, bias, group):
    scores = lax.dot_general(
        kv_ref[rows, lane_pair(group)],
        q_ref[group],
        (((1,), (1,)), ((), ())),
        preferred_element_type=jnp.float32,
    )
    return scores + bias


def lay_pieces(piece_refs, kv_ref):
    rows = piece_refs[0].shape[0]
    for i, piece_ref in enumerate(piece_refs):
        kv_ref[i * rows : (i + 1) * rows, :] = piece_ref[...]


def attend_kernel(base_ref, query_ref, *refs, half_rows):
    *piece_refs, q_ref, o_ref, lse_ref, kv_ref, bias_ref = refs
    lay_pieces(piece_refs, kv_ref)
    fill_bias(base_ref, query_ref, bias_ref, half_rows)
    wide = q_ref.shape[1]
    tiles = kv_ref.shape[0] // TILE
    for group in range(KEY_VALUE_HEADS):

        def step(tile, carry, group=group):
            top, total, mixed = carry
            rows = pl.ds(pl.multiple_of(tile * TILE, TILE), TILE)
            bias = jnp.concatenate([bias_ref[rows, :]] * (wide // LANES), axis=1)
            scores = tile_scores(kv_ref, rows, q_ref, bias, group)
            new_top = jnp.maximum(top, jnp.max(scores, axis=0, keepdims=True))
            factor = jnp.exp(top - new_top)
            weights = jnp.exp(scores - new_top)
            total = total * factor + jnp.sum(weights, axis=0, keepdims=True)
            mixed = mixed * factor + lax.dot_general(
                kv_ref[rows, lane_pair(KEY_VALUE_HEADS + group)],
                weights.astype(jnp.bfloat16),
                (((0,), (0,)), ((), ())),
                preferred_element_type=jnp.float32,
            )
            return new_top, total, mixed

        top, total, mixed = lax.fori_loop(
            0,
            tiles,
            step,
            (
                jnp.full((1, wide), MASK_FLOOR, jnp.float32),
                jnp.zeros((1, wide), jnp.float32),
                jnp.zeros((LANES, wide), jnp.float32),
            ),
        )
        side = (KEY_VALUE_HEADS + group) % 2 * HEAD_WIDTH
        o_ref[group] = (mixed / total)[side : side + HEAD_WIDTH]
        lse_ref[group] = top + jnp.log(total)


def backward_kernel(base_ref, query_ref, *refs, half_rows):
    pieces = (len(refs) - 8) // 2
    piece_refs, refs = refs[:pieces], refs[pieces:]
    (q_ref, do_ref, lse_ref, delta_ref), refs = refs[:4], refs[4:]
    out_refs, (dq_ref, kv_ref, dkv_ref, bias_ref) = refs[:pieces], refs[pieces:]
    lay_pieces(piece_refs, kv_ref)
    fill_bias(base_ref, query_ref, bias_ref, half_rows)
    wide = q_ref.shape[1]
    tiles = kv_ref.shape[0] // TILE
    dq_ref[...] = jnp.zeros_like(dq_ref)

    def step(tile, carry):
        rows = pl.ds(pl.multiple_of(tile * TILE, TILE), TILE)
        bias = jnp.concatenate([bias_ref[rows, :]] * (wide // LANES), axis=1)
        sums = [None] * KEY_VALUE_HEADS

        def collect(part, term):
            pair = part // 2
            sums[pair] = term if sums[pair] is None else sums[pair] + term

        for group in range(KEY_VALUE_HEADS):
            scores = tile_scores(kv_ref, rows, q_ref, bias, group)
            probs = jnp.exp(scores - lse_ref[group])
            grad_probs = lax.dot_general(
                kv_ref[rows, lane_pair(KEY_VALUE_HEADS + group)],
                do_ref[group],
                (((1,), (1,)), ((), ())),
                preferred_element_type=jnp.float32,
            )
            ds = (probs * (grad_probs - delta_ref[group])).astype(jnp.bfloat16)
            collect(
                KEY_VALUE_HEADS + group,
                jnp.dot(
                    probs.astype(jnp.bfloat16), do_ref[group], preferred_element_type=jnp.float32
                ),
            )
            collect(group, jnp.dot(ds, q_ref[group], preferred_element_type=jnp.float32))
            dq_ref[group] += lax.dot_general(
                kv_ref[rows, lane_pair(group)],
                ds,
                (((0,), (0,)), ((), ())),
                preferred_element_type=jnp.float32,
            )
        for pair in range(KEY_VALUE_HEADS):
            dkv_ref[rows, pair * LANES : (pair + 1) * LANES] = sums[pair].astype(jnp.bfloat16)
        return carry

    lax.fori_loop(0, tiles, step, 0)
    for i, out_ref in enumerate(out_refs):
        out_ref[...] = dkv_ref[i * out_ref.shape[0] : (i + 1) * out_ref.shape[0], :]


def in_vmem():
    return pl.BlockSpec(memory_space=pltpu.VMEM)


def in_smem():
    return pl.BlockSpec(memory_space=pltpu.SMEM)


def spread_heads(rows, offset):
    count = rows.shape[0]
    heads = rows.reshape(count, KEY_VALUE_HEADS, -1, HEAD_WIDTH).transpose(1, 2, 0, 3)
    heads = heads.reshape(KEY_VALUE_HEADS, -1, HEAD_WIDTH)
    blank = jnp.zeros_like(heads)
    left = jnp.concatenate([heads, blank], axis=2)
    right = jnp.concatenate([blank, heads], axis=2)
    side = (offset + jnp.arange(KEY_VALUE_HEADS, dtype=jnp.int32)) % 2
    return jnp.where(side[:, None, None] == 0, left, right)


def join_heads(heads, count):
    heads = heads.reshape(KEY_VALUE_HEADS, HEAD_WIDTH, -1, count)
    return heads.transpose(3, 0, 2, 1).reshape(count, QUERY_HEADS * HEAD_WIDTH)


def attend(bases, query_pos, key_value, queries, half_rows):
    groups, wide, lanes = queries.shape
    keys, lanes_all = sum(piece.shape[0] for piece in key_value), key_value[0].shape[1]
    return pl.pallas_call(
        functools.partial(attend_kernel, half_rows=half_rows),
        out_shape=(
            jax.ShapeDtypeStruct((groups, HEAD_WIDTH, wide), jnp.float32),
            jax.ShapeDtypeStruct((groups, 1, wide), jnp.float32),
        ),
        in_specs=[in_smem()] + [in_vmem()] * (2 + len(key_value)),
        out_specs=(in_vmem(), in_vmem()),
        scratch_shapes=[
            pltpu.VMEM((keys, lanes_all), jnp.bfloat16),
            pltpu.VMEM((keys, lanes), jnp.float32),
        ],
        compiler_params=pltpu.CompilerParams(vmem_limit_bytes=40 * 2**20),
        cost_estimate=pl.CostEstimate(
            flops=4 * groups * wide * lanes * keys,
            bytes_accessed=keys * 640 * 2,
            transcendentals=groups * wide * keys,
        ),
        name="attend",
    )(bases, query_pos, *key_value, queries)


def attend_backward(bases, query_pos, key_value, queries, head_grads, lse, delta, half_rows):
    groups, wide, lanes = queries.shape
    keys, lanes_all = sum(piece.shape[0] for piece in key_value), key_value[0].shape[1]
    return pl.pallas_call(
        functools.partial(backward_kernel, half_rows=half_rows),
        out_shape=(
            *[jax.ShapeDtypeStruct(piece.shape, jnp.bfloat16) for piece in key_value],
            jax.ShapeDtypeStruct((groups, lanes, wide), jnp.float32),
        ),
        in_specs=[in_smem()] + [in_vmem()] * (5 + len(key_value)),
        out_specs=(in_vmem(),) * (len(key_value) + 1),
        scratch_shapes=[
            pltpu.VMEM((keys, lanes_all), jnp.bfloat16),
            pltpu.VMEM((keys, lanes_all), jnp.bfloat16),
            pltpu.VMEM((keys, lanes), jnp.float32),
        ],
        compiler_params=pltpu.CompilerParams(vmem_limit_bytes=40 * 2**20),
        cost_estimate=pl.CostEstimate(
            flops=10 * groups * wide * lanes * keys,
            bytes_accessed=keys * 640 * 4,
            transcendentals=groups * wide * keys,
        ),
        name="attend_backward",
    )(bases, query_pos, *key_value, queries, head_grads, lse, delta)


def dot_nt(left, right):
    return lax.dot_general(
        left, right, (((1,), (1,)), ((), ())), preferred_element_type=jnp.float32
    )


def dot_tn(left, right):
    return lax.dot_general(
        left, right, (((0,), (0,)), ((), ())), preferred_element_type=jnp.float32
    )


def mlp_kernel(
    w_ref, x_ref, dy_ref, down_ref, dx_ref, term_ref, wg_ref, wu_ref, wd_ref, h_ref, dg_ref, du_ref
):
    blocks = w_ref.shape[0]
    slots = 2 * COLUMN_SLOT

    def unpack(i, carry):
        units = pl.ds(pl.multiple_of(i * UNIT_SLOT, 16), UNIT_SLOT)
        wg_ref[units, :] = w_ref[i, :UNIT_SLOT]
        wu_ref[units, :] = w_ref[i, UNIT_SLOT : 2 * UNIT_SLOT]
        first = 2 * UNIT_SLOT
        for row, count, block, start, group in fold_pieces():
            wd_ref[
                pl.ds(pl.multiple_of(i * slots + row, 16), count),
                block * SLOT_LANES : (block + 1) * SLOT_LANES,
            ] = w_ref[
                i,
                first + start : first + start + count,
                group * SLOT_LANES : (group + 1) * SLOT_LANES,
            ]
        return carry

    lax.fori_loop(0, blocks, unpack, 0)
    step_rows = 256
    for step in range(x_ref.shape[0] // step_rows):
        rows = slice(step * step_rows, (step + 1) * step_rows)
        x = x_ref[rows]
        dy = dy_ref[rows]
        gate = dot_nt(x, wg_ref[...])
        up = dot_nt(x, wu_ref[...])
        sigmoid = jax.nn.sigmoid(gate)
        silu = gate * sigmoid
        hidden = (silu * up).astype(jnp.bfloat16)
        h_ref[rows] = hidden
        down_ref[rows] = dot_nt(hidden, wd_ref[...]).astype(jnp.bfloat16)
        dh = jnp.dot(dy, wd_ref[...], preferred_element_type=jnp.float32)
        dgate = (dh * up * sigmoid * (1.0 + gate * (1.0 - sigmoid))).astype(jnp.bfloat16)
        dup = (dh * silu).astype(jnp.bfloat16)
        dg_ref[rows] = dgate
        du_ref[rows] = dup
        dx = jnp.dot(dgate, wg_ref[...], preferred_element_type=jnp.float32)
        dx = dx + jnp.dot(dup, wu_ref[...], preferred_element_type=jnp.float32)
        dx_ref[rows] = dx.astype(jnp.bfloat16)
    per = 8
    for part in range(blocks // per):
        lanes = slice(part * per * UNIT_SLOT, (part + 1) * per * UNIT_SLOT)
        for at, grads in ((0, dg_ref), (UNIT_SLOT, du_ref)):
            term = dot_tn(grads[:, lanes], x_ref[...]).astype(jnp.bfloat16)
            for i in range(per):
                term_ref[part * per + i, at : at + UNIT_SLOT] = term[
                    i * UNIT_SLOT : (i + 1) * UNIT_SLOT
                ]
    per = 4
    for part in range(blocks // per):
        lanes = slice(part * per * slots, (part + 1) * per * slots)
        term = dot_tn(dy_ref[:, lanes], h_ref[...]).astype(jnp.bfloat16)
        for i in range(per):
            for row, count, block, start, group in fold_pieces():
                term_ref[
                    part * per + i,
                    2 * UNIT_SLOT + start : 2 * UNIT_SLOT + start + count,
                    group * SLOT_LANES : (group + 1) * SLOT_LANES,
                ] = term[
                    i * slots + row : i * slots + row + count,
                    block * SLOT_LANES : (block + 1) * SLOT_LANES,
                ]


def query_kernel(
    lanes_ref,
    cos_ref,
    sin_ref,
    order_ref,
    branch_ref,
    h_own_ref,
    h_other_ref,
    a_own_ref,
    a_other_ref,
    w_own_ref,
    w_other_ref,
    own_ref,
    other_ref,
    back_ref,
    dq_ref,
    *,
    scale_factor,
):
    half = HEAD_WIDTH // 2
    cos = cos_ref[...]
    sin = sin_ref[...]
    tokens = cos.shape[1]
    heads = lanes_ref.shape[2] // tokens
    for group in range(KEY_VALUE_HEADS):
        at = group % 2 * HEAD_WIDTH
        for head in range(heads):
            lanes = slice(head * tokens, (head + 1) * tokens)
            top = lanes_ref[group, at : at + half, lanes] * scale_factor
            low = lanes_ref[group, at + half : at + HEAD_WIDTH, lanes] * scale_factor
            row = (group * heads + head) * HEAD_WIDTH
            dq_ref[row : row + half] = (top * cos + low * sin).astype(jnp.bfloat16)
            dq_ref[row + half : row + HEAD_WIDTH] = (low * cos - top * sin).astype(jnp.bfloat16)
    slots = dot_tn(order_ref[...], dq_ref[...]).astype(jnp.bfloat16)
    cut = h_own_ref.shape[1]
    sides = (
        (own_ref, h_own_ref, a_own_ref, w_own_ref),
        (other_ref, h_other_ref, a_other_ref, w_other_ref),
    )
    for i, (out_ref, h_ref, a_ref, w_ref) in enumerate(sides):
        out_ref[:, :cut] = jnp.dot(
            slots, h_ref[...], preferred_element_type=jnp.float32
        ).astype(jnp.bfloat16)
        out_ref[:, cut:] = dot_tn(branch_ref[...], a_ref[...]).astype(jnp.bfloat16)
        back_ref[i] = dot_tn(slots, w_ref[:, :cut])


def query_terms(grad_lanes, cosine, sine, order, branch, rows, mixed, weights, scale_factor):
    columns, slots = order.shape
    count, cut = rows[0].shape
    return pl.pallas_call(
        functools.partial(query_kernel, scale_factor=scale_factor),
        out_shape=(
            jax.ShapeDtypeStruct((slots, 2 * cut), jnp.bfloat16),
            jax.ShapeDtypeStruct((slots, 2 * cut), jnp.bfloat16),
            jax.ShapeDtypeStruct((2, count, cut), jnp.float32),
        ),
        in_specs=[in_vmem()] * 11,
        out_specs=(in_vmem(),) * 3,
        scratch_shapes=[pltpu.VMEM((columns, count), jnp.bfloat16)],
        compiler_params=pltpu.CompilerParams(vmem_limit_bytes=40 * 2**20),
        cost_estimate=pl.CostEstimate(
            flops=2 * 10**10, bytes_accessed=4 * 10**7, transcendentals=0
        ),
        name="query_terms",
    )(grad_lanes, cosine, sine, order, branch, *rows, *mixed, *weights)


def feed_forward(weights, rows, grads):
    blocks = weights.shape[0]
    count, wide = rows.shape
    units = blocks * UNIT_SLOT
    slots = blocks * 2 * COLUMN_SLOT
    return pl.pallas_call(
        mlp_kernel,
        out_shape=(
            jax.ShapeDtypeStruct((count, slots), jnp.bfloat16),
            jax.ShapeDtypeStruct((count, wide), jnp.bfloat16),
            jax.ShapeDtypeStruct((blocks, MLP_ROWS, wide), jnp.bfloat16),
        ),
        in_specs=[in_vmem()] * 3,
        out_specs=(in_vmem(),) * 3,
        scratch_shapes=[
            pltpu.VMEM((units, wide), jnp.bfloat16),
            pltpu.VMEM((units, wide), jnp.bfloat16),
            pltpu.VMEM((slots, units), jnp.bfloat16),
            pltpu.VMEM((count, units), jnp.bfloat16),
            pltpu.VMEM((count, units), jnp.bfloat16),
            pltpu.VMEM((count, units), jnp.bfloat16),
        ],
        compiler_params=pltpu.CompilerParams(vmem_limit_bytes=48 * 2**20),
        cost_estimate=pl.CostEstimate(
            flops=18 * count * units * wide,
            bytes_accessed=2 * weights.size * 2,
            transcendentals=count * units,
        ),
        name="feed_forward",
    )(weights, rows, grads)


def body(
    tokens,
    pair_table,
    gain_attn,
    w_query,
    w_key,
    w_value,
    w_out,
    gain_mlp,
    w_gate,
    w_up,
    w_down,
    cotangent,
):
    device_rows, columns = tokens.shape[1:]
    half_rows = device_rows // 2
    width = HEAD_WIDTH * KEY_VALUE_HEADS
    query_per_group = QUERY_HEADS // KEY_VALUE_HEADS
    scale_factor = 1.0 / math.sqrt(HEAD_WIDTH)
    part, each = w_query.shape
    each_key = w_key.shape[1]
    each_unit = w_gate.shape[1] // 4
    unit_rows = -(-each_unit // 8) * 8
    unit_lanes = 4 * UNIT_SLOT
    slot = COLUMN_SLOT
    first_core = lax.axis_index("core") == 0
    within = jnp.arange(half_rows, dtype=jnp.int32)
    blocks = block_table(pair_table)
    chunk_count = blocks.shape[0]
    own_pos = jnp.concatenate(
        [blocks[0] * half_rows + within, blocks[chunk_count // 2] * half_rows + within]
    )
    cosine_lookup, sine_lookup = rope_tables(own_pos, HEAD_WIDTH)
    slot_column, slot_used = column_slots(columns)
    head_order = one_hot(slot_column, columns, slot_used)
    order = one_hot(wide_place(slot_column, part), 4 * SLOT_LANES, slot_used)
    unit_order = hidden_order(w_down.shape[0])
    key_rows = -(-2 * each_key // 8) * 8
    key_order = key_value_order(width, key_rows)

    key_chunk = pad_to(jnp.concatenate([w_key.T, w_value.T], axis=0), key_rows, SLOT_LANES)
    key_all = exchange(jnp.broadcast_to(key_chunk[None], (128,) + key_chunk.shape), AXES)

    down_units = jnp.einsum(
        "fd,fu->du", w_down, unit_order, preferred_element_type=jnp.float32
    ).astype(jnp.bfloat16)
    shared = [pad_to(w_query.T, slot, SLOT_LANES), pad_to(w_out.T, slot, SLOT_LANES)]

    def for_fsdp(fsdp):
        units = slice(fsdp * each_unit, (fsdp + 1) * each_unit)
        return jnp.concatenate(
            shared
            + [
                pad_to(w_gate.T[units], unit_rows, SLOT_LANES),
                pad_to(w_up.T[units], unit_rows, SLOT_LANES),
                pad_to(
                    down_units[:, fsdp * unit_lanes : (fsdp + 1) * unit_lanes], slot, SLOT_LANES
                ),
            ],
            axis=0,
        )

    chunk = jnp.stack([for_fsdp(i) for i in range(4)])
    chunk, key_all = lax.optimization_barrier((chunk, key_all))
    near = exchange(jnp.concatenate([chunk, chunk], axis=0), NEAR)
    near = near.reshape((2, 4) + near.shape[1:])
    mine = jnp.where(first_core, near[:, 0::2, : 2 * slot], near[:, 1::2, : 2 * slot])
    shard_attn = jnp.concatenate(
        [mine[:, i, j * slot : (j + 1) * slot] for j in range(2) for i in range(2)], axis=2
    ).reshape(2 * slot, 4 * SLOT_LANES)

    def lay_units(start):
        cut = near[:, :, start : start + each_unit]
        rows = [jnp.concatenate([cut[x, i] for i in range(4)], axis=1) for x in range(2)]
        return pad_to(jnp.concatenate(rows, axis=0), UNIT_SLOT, 4 * SLOT_LANES)

    shard_down = near[:, :, 2 * slot + 2 * unit_rows :, :unit_lanes]
    shard_down = jnp.concatenate([shard_down[:, i] for i in range(4)], axis=2)
    attn_own = lax.all_gather(shard_attn[None], RING, axis=0, tiled=True)
    attn_own = attn_own.reshape(-1, 4 * SLOT_LANES)
    packed = jnp.concatenate(
        [
            lay_units(2 * slot),
            lay_units(2 * slot + unit_rows),
            fold(shard_down.reshape(2 * slot, 4 * unit_lanes)),
        ],
        axis=0,
    )
    def forth_halves(rows, halves):
        own, other = core_halves(rows)
        return forth(own, halves[0]) + forth(other, halves[1])

    def back_halves(grads, halves):
        return join_core_halves(back(grads, halves[0]), back(grads, halves[1]))

    key_all = key_all.reshape(32, 4, key_rows, SLOT_LANES)
    key_value_w = [key_all[:, i].reshape(-1, SLOT_LANES) for i in range(4)]

    def mean_of(rows):
        return jnp.sum(rows, axis=-1, keepdims=True) / columns

    wide_gain_attn = widen(gain_attn[None], part)
    wide_gain_mlp = widen(gain_mlp[None], part)
    inputs = widen(tokens[0].astype(jnp.float32), part)
    inverse_one = lax.rsqrt(mean_of(inputs * inputs) + EPSILON)
    normed_one = inputs * inverse_one
    rounded_one = (normed_one * wide_gain_attn).astype(jnp.bfloat16)
    key_value_raw = sum(
        forth(rows, weights) for rows, weights in zip(lane_parts(rounded_one), key_value_w)
    )
    key_value_raw = unpermute(key_value_raw, key_order)
    key_local = (
        apply_rotary(
            key_value_raw[:, :width].reshape(device_rows, KEY_VALUE_HEADS, HEAD_WIDTH),
            cosine_lookup,
            sine_lookup,
        )
        .astype(jnp.bfloat16)
        .reshape(device_rows, width)
    )
    key_value = jnp.concatenate([key_local, key_value_raw[:, width:].astype(jnp.bfloat16)], axis=1)
    other = shift(key_value, "xl", 1)
    low_rows = jnp.concatenate([key_value[:half_rows], other[:half_rows]], axis=0)
    high_rows = jnp.concatenate([key_value[half_rows:], other[half_rows:]], axis=0)
    low_rows = jnp.concatenate(ring_gather(low_rows, "z"), axis=0)
    high_rows = jnp.concatenate(ring_gather(high_rows, "y"), axis=0)
    grad_result = widen(cotangent[0], part)
    grad_slots = from_four(permute(grad_result, order))
    low_rows, high_rows, grad_slots = lax.optimization_barrier((low_rows, high_rows, grad_slots))
    key_value_all = ring_gather(low_rows, "y") + ring_gather(high_rows, "z")
    key_value_all, attn_own, packed = lax.optimization_barrier((key_value_all, attn_own, packed))
    packed = lax.all_gather(packed[None], RING, axis=0, tiled=True)
    attn_w = (attn_own, shift(attn_own, "core", 1))
    query_w = [half[:, : 2 * SLOT_LANES] for half in attn_w]
    out_w = [half[:, 2 * SLOT_LANES :] for half in attn_w]
    query_raw = unpermute(forth_halves(rounded_one, query_w), head_order).reshape(
        device_rows, QUERY_HEADS, HEAD_WIDTH
    )
    query_heads = apply_rotary(query_raw, cosine_lookup, sine_lookup).astype(jnp.bfloat16)
    queries = spread_heads(
        query_heads.reshape(device_rows, QUERY_HEADS * HEAD_WIDTH)
        * jnp.asarray(scale_factor, jnp.bfloat16),
        0,
    )
    bases = blocks * half_rows
    query_pos = own_pos[None, :]
    mixed, log_total = attend(bases, query_pos, key_value_all, queries, half_rows)
    mixture = join_heads(mixed, device_rows)
    attended = mixture.astype(jnp.bfloat16)
    wide_attended = widen(attended, part)
    middle = inputs + unpermute(forth_halves(wide_attended, out_w), order)
    inverse_two = lax.rsqrt(mean_of(middle * middle) + EPSILON)
    normed_two = middle * inverse_two
    rounded_two = (normed_two * wide_gain_mlp).astype(jnp.bfloat16)
    down_sums, unit_sums, ring_terms = feed_forward(
        packed, from_four(rounded_two), grad_slots
    )
    sums = to_four(jnp.concatenate([unit_sums, down_sums], axis=1))
    grad_normed_two = sums[:, : 4 * SLOT_LANES]
    down_sums = sums[:, 4 * SLOT_LANES :]
    ring_terms = lax.psum_scatter(ring_terms, "y", scatter_dimension=0, tiled=True)
    grad_gain_mlp = jnp.sum(grad_normed_two * normed_two, axis=0)
    scaled_two = grad_normed_two * wide_gain_mlp
    grad_middle = grad_result.astype(jnp.float32) + inverse_two * (
        scaled_two - normed_two * mean_of(scaled_two * normed_two)
    )
    grad_branch = permute(grad_middle.astype(jnp.bfloat16), order)
    attended_gradient = narrow(back_halves(grad_branch, out_w).astype(jnp.bfloat16), part)
    delta_rows = jnp.sum(
        (attended_gradient.astype(jnp.float32) * mixture).reshape(
            device_rows, KEY_VALUE_HEADS, query_per_group, HEAD_WIDTH
        ),
        axis=-1,
    )
    delta_rows = delta_rows.transpose(1, 2, 0).reshape(KEY_VALUE_HEADS, 1, -1)
    *key_value_terms, grad_query_lanes = attend_backward(
        bases,
        query_pos,
        key_value_all,
        queries,
        spread_heads(attended_gradient, KEY_VALUE_HEADS),
        log_total,
        delta_rows,
        half_rows,
    )
    key_value_terms, ring_terms = lax.optimization_barrier((key_value_terms, ring_terms))
    low_arrived = ring_sends(key_value_terms[:4], "y")
    high_arrived = ring_sends(key_value_terms[4:], "z")
    low_arrived, high_arrived = lax.optimization_barrier((low_arrived, high_arrived))

    *attn_terms, query_back = query_terms(
        grad_query_lanes,
        cosine_lookup[:, 0, : HEAD_WIDTH // 2].T,
        sine_lookup[:, 0, : HEAD_WIDTH // 2].T,
        head_order,
        grad_branch,
        core_halves(rounded_one),
        core_halves(wide_attended),
        attn_w,
        scale_factor,
    )
    attn_terms = add(attn_terms[0], shift(attn_terms[1], "core", 1))
    attn_terms = lax.psum_scatter(
        attn_terms.reshape(16, ATTN_ROWS, -1), "y", scatter_dimension=0, tiled=True
    )
    key_value_near = jnp.concatenate(
        [
            ring_scatter(jnp.split(ring_sum(low_arrived), 4, axis=0), "z"),
            ring_scatter(jnp.split(ring_sum(high_arrived), 4, axis=0), "y"),
        ],
        axis=0,
    )
    key_value_near, attn_terms, ring_terms = lax.optimization_barrier(
        (key_value_near, attn_terms, ring_terms)
    )
    key_value_near = key_value_near.reshape(2, 2, half_rows, 2 * width)
    key_value_gradient = add(
        key_value_near[:, 0].reshape(device_rows, -1),
        shift(key_value_near[:, 1].reshape(device_rows, -1), "xl", 1),
    )
    key_value_gradient, down_sums = lax.optimization_barrier((key_value_gradient, down_sums))
    result = (middle + unpermute(down_sums, order)).astype(jnp.bfloat16)
    grad_key_rows = (
        inverse_rotary(
            key_value_gradient[:, :width]
            .astype(jnp.float32)
            .reshape(device_rows, KEY_VALUE_HEADS, HEAD_WIDTH),
            cosine_lookup,
            sine_lookup,
        )
        .reshape(device_rows, width)
        .astype(jnp.bfloat16)
    )
    grad_key_slots = permute(
        jnp.concatenate([grad_key_rows, key_value_gradient[:, width:]], axis=1), key_order
    )
    grad_normed_one = join_core_halves(query_back[0], query_back[1]) + jnp.concatenate(
        [back(grad_key_slots, weights) for weights in key_value_w], axis=1
    )
    scaled_one = grad_normed_one * wide_gain_attn
    grad_inputs = grad_middle + inverse_one * (
        scaled_one - normed_one * mean_of(scaled_one * normed_one)
    )

    key_terms = jnp.stack(
        [
            weight_term(grad_key_slots, rows).reshape(32, key_rows, SLOT_LANES)
            for rows in lane_parts(rounded_one)
        ],
        axis=1,
    ).reshape(128, key_rows, SLOT_LANES)
    gain_terms = gain_rows(jnp.sum(grad_normed_one * normed_one, axis=0))
    key_terms = jnp.concatenate([key_terms, gain_terms, gain_rows(grad_gain_mlp)], axis=1)
    ring_terms = jnp.concatenate([attn_terms, ring_terms], axis=1)
    ring_terms = ring_scatter(pick(ring_terms, "z", 0), "z")
    gate_at = ATTN_ROWS
    up_at = gate_at + UNIT_SLOT
    down_terms = unfold(ring_terms[up_at + UNIT_SLOT :])

    def chunk_for(xl, fsdp):
        lanes = slice(fsdp * SLOT_LANES, (fsdp + 1) * SLOT_LANES)
        at = fsdp // 2 * SLOT_LANES
        query_lanes = slice(at, at + SLOT_LANES)
        out_lanes = slice(2 * SLOT_LANES + at, 3 * SLOT_LANES + at)
        slots = slice(xl * slot, (xl + 1) * slot)
        units = xl * each_unit
        return jnp.concatenate(
            [
                ring_terms[slots, query_lanes],
                ring_terms[slots, out_lanes],
                pad_to(
                    ring_terms[gate_at + units : gate_at + units + each_unit, lanes],
                    unit_rows,
                    SLOT_LANES,
                ),
                pad_to(
                    ring_terms[up_at + units : up_at + units + each_unit, lanes],
                    unit_rows,
                    SLOT_LANES,
                ),
                pad_to(
                    down_terms[slots, fsdp * unit_lanes : (fsdp + 1) * unit_lanes],
                    slot,
                    SLOT_LANES,
                ),
            ],
            axis=0,
        )

    chunks = jnp.stack([chunk_for(xl, fsdp) for xl in range(2) for fsdp in range(4)])
    key_sums = exchange(key_terms, AXES)
    chunks, key_sums = lax.optimization_barrier((chunks, key_sums))
    near = exchange(chunks, NEAR).astype(jnp.float32)
    key_sums = jnp.sum(key_sums.astype(jnp.float32), axis=0)
    near = near.reshape((2, 4) + near.shape[1:]).sum(axis=0)
    attn_sums = near[:, : 2 * slot]
    attn_sums = jnp.where(
        first_core, attn_sums[0] + attn_sums[2], attn_sums[1] + attn_sums[3]
    )
    grad_query = attn_sums[:each, :part]
    grad_out = attn_sums[slot : slot + each, :part]
    at = 2 * slot
    grad_gate = near[:, at : at + each_unit, :part].reshape(-1, part)
    at = at + unit_rows
    grad_up = near[:, at : at + each_unit, :part].reshape(-1, part)
    at = at + unit_rows
    grad_down = jnp.concatenate([near[i, at:, :unit_lanes] for i in range(4)], axis=1)
    grad_down = jnp.einsum(
        "du,fu->fd",
        grad_down,
        unit_order.astype(jnp.float32),
        precision=EXACT,
        preferred_element_type=jnp.float32,
    )

    grad_key = key_sums[:each_key, :part]
    grad_value = key_sums[each_key : 2 * each_key, :part]
    grad_gain_attn = joined_gain(key_sums[key_rows : key_rows + 8], part)
    grad_gain_mlp = joined_gain(key_sums[key_rows + 8 :], part)

    return (
        narrow(result, part)[None],
        narrow(grad_inputs, part)[None],
        grad_gain_attn,
        grad_query.T,
        grad_key.T,
        grad_value.T,
        grad_out.T,
        grad_gain_mlp,
        grad_gate.T,
        grad_up.T,
        grad_down[:, :each],
    )


def solution(mesh):
    grid = mesh.devices.reshape(4, 2, 4, 2, 2)
    fine = jax.sharding.Mesh(grid, AXES)
    rows = P(FSDP, CTX, None)
    weight = P(FSDP, CTX)
    return jax.shard_map(
        body,
        mesh=fine,
        in_specs=(
            rows,
            P(),
            P(),
            weight,
            weight,
            weight,
            weight,
            P(),
            weight,
            weight,
            weight,
            rows,
        ),
        out_specs=(
            rows,
            rows,
            P(),
            weight,
            weight,
            weight,
            weight,
            P(),
            weight,
            weight,
            weight,
        ),
        check_vma=False,
    )
```
